32 devices in a mesh: tok: 8 (over z, x), mdl: 4 (over y, core).
Axes of the slice: x: 2, y: 2, z: 4, core: 2. Of those that a mesh axis runs over, the one named last changes fastest.
Arguments:
- tok_grad: bfloat16 [16384, 2048], P('tok', 'mdl'), may hold values from -0.119628906 to 0.119628906
- occurrence: int32 [16384], P('tok'), may hold values from 0 to 1023
- owned: int32 [1024], replicated, may hold values from 0 to 1023, each once
- token_ids: int32 [1024, 8], P('tok'), may hold values from 0 to 31999, as said below
- embeds: bfloat16 [1024, 8, 2048], P('tok', None, 'mdl'), may hold values from -6 to 6
- gain: float32 [2048], replicated, may hold values from 0.5 to 1.5
- w_query: bfloat16 [2048, 2048], P(None, 'mdl'), may hold values from -0.125 to 0.125
- w_key: bfloat16 [2048, 2048], P(None, 'mdl'), may hold values from -0.125 to 0.125
- w_value: bfloat16 [2048, 2048], P(None, 'mdl'), may hold values from -0.125 to 0.125
- w_out: bfloat16 [2048, 2048], P('mdl'), may hold values from -0.125 to 0.125
Outputs:
- embed_grad: bfloat16 [1024, 8, 2048], P('tok', None, 'mdl')
- query_grad: float32 [2048, 2048], P('tok', 'mdl')
- key_grad: float32 [2048, 2048], P('tok', 'mdl')
- value_grad: float32 [2048, 2048], P('tok', 'mdl')
- out_grad: float32 [2048, 2048], P('mdl', 'tok')
The draws below stay inside these ranges and needn't reach their ends.
Inputs may be any that keep to these rules, and one draw needn't show every extreme that they name: `token_ids`: in each row the nonzero ids come first, then zeros; every row has at least one nonzero id, and some row is full and some has one token.
All inputs are finite; a program needn't handle non-finite values.
Results may differ from the reference program's by a relative error of at most 0.01.
Values may be sent and summed in bfloat16 or wider, within the bound.
No kernel may reach another device: no remote copies, remote signals or barrier semaphores. Data moves between devices by JAX's collectives and lax.ppermute only.
A program may use at most 128 MiB of HBM per device.

```python
import math
import jax
import jax.numpy as jnp
import numpy as np
from jax import lax

D = 2048
HEAD = 128
FLEN = 8
VOCAB = 32000
FGRAMS = 1024
TOKENS = 16384


def draw_token_ids(key, part):
    key = jax.random.fold_in(key, 7)
    key_len, key_ids = jax.random.split(key)
    length = jax.random.randint(key_len, (FGRAMS,), 1, FLEN + 1)
    length = length.at[0].set(FLEN).at[1].set(1)
    ids = jax.random.randint(key_ids, (FGRAMS, FLEN), 1, VOCAB)
    positions = jnp.arange(FLEN, dtype=jnp.int32)
    return jnp.where(positions[None, :] < length[:, None], ids, 0).astype(jnp.int32)


def set_ends(values, key, low, largest):
    longest = values.shape.index(max(values.shape))
    spots = []
    for shift in (0, 1):
        where = [jax.random.randint(jax.random.fold_in(key, axis), (), 0, length) for axis, length in enumerate(values.shape)]
        where[longest] = (where[longest] + shift) % values.shape[longest]
        spots.append(tuple(where))
    return values.at[spots[0]].set(low).at[spots[1]].set(largest)


def steps_of(own_key, dims, shards, smallest, top_value):
    loudness = 1.0
    for position, parts in shards:
        draws = jax.random.uniform(jax.random.fold_in(jax.random.fold_in(own_key, 6), position), (parts,), jnp.float32, smallest / len(shards), top_value / len(shards))
        loudness = loudness * jnp.repeat(jnp.exp(draws), dims[position] // parts).reshape((-1,) + (1,) * (len(dims) - 1 - position))
    return loudness


def rank_table(count, lean):
    portions = [(1 << 20) // math.isqrt(standing ** lean) + 1 for standing in range(1, count + 1)]
    deviation = 1 + sum(portions) // (1 << 30)
    return np.cumsum(np.array([max(1, weight // deviation) for weight in portions]))


def ranked(own_key, shape, number_of, lean):
    grid = rank_table(number_of, lean)
    lot = jax.random.randint(jax.random.fold_in(own_key, 1), shape, 0, int(grid[number_of - 1]))
    rank = jnp.searchsorted(jnp.asarray(grid, jnp.int32), lot, side="right")
    return jax.random.permutation(jax.random.fold_in(own_key, 2), number_of)[rank].astype(jnp.int32)


def normal_values(own_key, extent, deviation, limit, shards=(), kind=jnp.bfloat16):
    level = steps_of(own_key, extent, shards, -0.22, 0.18) if shards else 1.0
    values = jax.random.normal(own_key, extent, jnp.float32) * deviation * level
    return jnp.minimum(jnp.maximum(values, -limit), limit).astype(kind)


def setup_inputs(seed: int = 0) -> dict:
    streams_of = jax.random.split(jax.random.key(seed), 11)
    return {
        "tok_grad": normal_values(streams_of[0], (TOKENS, D), 0.02, 0.119628906, ((0, 8), (1, 4))),
        "occurrence": set_ends(ranked(streams_of[1], (TOKENS,), FGRAMS, 1), jax.random.fold_in(streams_of[1], 3), 0, FGRAMS - 1).astype(jnp.int32),
        "owned": jax.random.permutation(streams_of[2], FGRAMS).astype(jnp.int32),
        "token_ids": draw_token_ids(jax.random.fold_in(streams_of[10], 71), 0),
        "embeds": normal_values(streams_of[4], (FGRAMS, FLEN, D), 1.0, 6.0, ((0, 8), (2, 4))),
        "gain": jnp.clip(1.0 + 0.1 * jax.random.normal(streams_of[5], (D,), jnp.float32), 0.5, 1.5),
        "w_query": normal_values(streams_of[6], (D, D), D ** -0.5, 0.125, ((1, 4),)),
        "w_key": normal_values(streams_of[7], (D, D), D ** -0.5, 0.125, ((1, 4),)),
        "w_value": normal_values(streams_of[8], (D, D), D ** -0.5, 0.125, ((1, 4),)),
        "w_out": normal_values(streams_of[9], (D, D), D ** -0.5, 0.125, ((0, 4),)),
    }


def reference(tok_grad, occurrence, owned, token_ids, embeds, gain, w_query, w_key, w_value, w_out):
    f32 = jnp.float32
    bf16 = jnp.bfloat16
    heads = D // HEAD
    scale = 1.0 / HEAD ** 0.5
    rank = jnp.zeros((FGRAMS,), jnp.int32).at[owned].set(jnp.arange(FGRAMS, dtype=jnp.int32))
    target = rank[occurrence]
    fgram_sum = jax.ops.segment_sum(tok_grad.astype(f32), target, FGRAMS)
    fgram_grad = fgram_sum.astype(bf16)
    length = lax.optimization_barrier(jnp.sum((token_ids != 0).astype(jnp.int32), axis=1))
    positions = jnp.arange(FLEN, dtype=jnp.int32)
    lastmask = positions[None, :] == (length - 1)[:, None]
    keymask = (positions[None, :] < length[:, None]).astype(f32)
    xfull = embeds.astype(f32)
    recip = lax.rsqrt(lax.optimization_barrier(jnp.mean(xfull * xfull, axis=-1)) + 1e-06)
    normed = (xfull * recip[..., None] * gain).astype(bf16)
    normed_last = lax.optimization_barrier(jnp.sum(jnp.where(lastmask[..., None], normed.astype(f32), 0.0), axis=1)).astype(bf16)
    rows = normed.reshape(FGRAMS * FLEN, D)
    keys = jnp.dot(rows, w_key, preferred_element_type=f32).astype(bf16).reshape(FGRAMS, FLEN, heads, HEAD)
    values = jnp.dot(rows, w_value, preferred_element_type=f32).astype(bf16).reshape(FGRAMS, FLEN, heads, HEAD)
    query = jnp.dot(normed_last, w_query, preferred_element_type=f32).astype(bf16).reshape(FGRAMS, heads, HEAD)
    keys32 = keys.astype(f32)
    values32 = values.astype(f32)
    query32 = query.astype(f32)
    scores = jnp.einsum('fhd,fjhd->fhj', query32, keys32) * scale
    expo = jnp.exp(scores) * keymask[:, None, :]
    probs = expo / lax.optimization_barrier(jnp.sum(expo, axis=-1, keepdims=True))
    probs_b = probs.astype(bf16).astype(f32)
    attended = jnp.einsum('fhj,fjhd->fhd', probs_b, values32).astype(bf16).reshape(FGRAMS, D)
    d_att = jnp.dot(fgram_grad, w_out.T, preferred_element_type=f32).reshape(FGRAMS, heads, HEAD)
    d_prob = jnp.einsum('fhd,fjhd->fhj', d_att, values32)
    d_score = probs * (d_prob - lax.optimization_barrier(jnp.sum(probs * d_prob, axis=-1, keepdims=True))) * scale
    d_query = jnp.einsum('fhj,fjhd->fhd', d_score, keys32).astype(bf16).reshape(FGRAMS, D)
    d_key = jnp.einsum('fhj,fhd->fjhd', d_score, query32).astype(bf16).reshape(FGRAMS * FLEN, D)
    d_value = jnp.einsum('fhj,fhd->fjhd', probs_b, d_att).astype(bf16).reshape(FGRAMS * FLEN, D)
    query_grad = jnp.dot(normed_last.T, d_query, preferred_element_type=f32)
    key_grad = jnp.dot(rows.T, d_key, preferred_element_type=f32)
    value_grad = jnp.dot(rows.T, d_value, preferred_element_type=f32)
    out_grad = jnp.dot(attended.T, fgram_grad, preferred_element_type=f32)
    d_normed = jnp.dot(d_key, w_key.T, preferred_element_type=f32) + jnp.dot(d_value, w_value.T, preferred_element_type=f32)
    d_normed = d_normed.reshape(FGRAMS, FLEN, D)
    from_query = jnp.dot(d_query, w_query.T, preferred_element_type=f32)
    d_normed = d_normed + jnp.where(lastmask[..., None], from_query[:, None, :], 0.0)
    scaled = d_normed * gain
    product = lax.optimization_barrier(jnp.mean(xfull * scaled, axis=-1))
    result = recip[..., None] * scaled - xfull * (recip ** 3 * product)[..., None]
    result = result + jnp.where(lastmask[..., None], fgram_grad.astype(f32)[:, None, :], 0.0)
    embed_grad = result.astype(bf16)
    return (embed_grad, query_grad, key_grad, value_grad, out_grad)
```

```python
import functools

import jax
import jax.numpy as jnp
from jax import lax
from jax.experimental import pallas as pl
from jax.experimental.pallas import tpu as pltpu
from jax.sharding import PartitionSpec as P

HEAD = 128
BF = jnp.bfloat16
F32 = jnp.float32
VMEM = pl.BlockSpec(memory_space=pltpu.VMEM)
SMEM = pl.BlockSpec(memory_space=pltpu.SMEM)
LIMIT = 56 * 2**20


def dot(left, right):
    return jnp.dot(left, right, preferred_element_type=F32)


def tdot(left, right):
    return lax.dot_general(left, right, (((0,), (0,)), ((), ())), preferred_element_type=F32)


def rdot(left, right):
    return lax.dot_general(left, right, (((1,), (1,)), ((), ())), preferred_element_type=F32)


def call(body, ins, outs, scratch=(), smem=1, flops=0):
    return pl.pallas_call(
        body,
        in_specs=[SMEM] * smem + [VMEM] * (len(ins) - smem),
        out_specs=[VMEM] * len(outs),
        out_shape=[jax.ShapeDtypeStruct(s, t) for s, t in outs],
        scratch_shapes=list(scratch),
        compiler_params=pltpu.CompilerParams(vmem_limit_bytes=LIMIT),
    )(*ins)


def sums_kernel(idx, owned, occ, grads, out):
    onehot = jnp.where(owned[...] == occ[...], 1.0, 0.0).astype(BF)
    out[...] = dot(onehot, grads[...]).astype(out.dtype)


def partial_sums(idx, owned, occ, grads, n_out, f_dev, other, dtype):
    tokens, cols = grads.shape

    def owner(k, idx):
        z, x = idx[1], idx[2]
        side = 1 - x if other else x
        return lax.rem(z + k, n_out) * 2 + side

    return pl.pallas_call(
        sums_kernel,
        grid_spec=pltpu.PrefetchScalarGridSpec(
            num_scalar_prefetch=1,
            grid=(n_out,),
            in_specs=[
                pl.BlockSpec((f_dev, 1), lambda k, idx: (owner(k, idx), 0)),
                pl.BlockSpec((1, tokens), lambda k, idx: (0, 0)),
                pl.BlockSpec((tokens, cols), lambda k, idx: (0, 0)),
            ],
            out_specs=pl.BlockSpec((f_dev, cols), lambda k, idx: (k, 0)),
        ),
        out_shape=jax.ShapeDtypeStruct((n_out * f_dev, cols), dtype),
        compiler_params=pltpu.CompilerParams(vmem_limit_bytes=LIMIT),
    )(idx, owned, occ, grads)


def norm_kernel(near, idx, x0, x1, x2, x3, gain, normed, recip, *sends):
    m, z, x = idx[0], idx[1], idx[2]
    blocks = (x0, x1, x2, x3)
    rows, cols = x0.shape
    width = 4 * cols
    tile = 128

    def step(i, carry):
        at = pl.ds(pl.multiple_of(i * tile, tile), tile)
        total = jnp.zeros((tile, 1), F32)
        for block in blocks:
            part = block[at, :].astype(F32)
            total = total + jnp.sum(part * part, axis=1, keepdims=True)
        r = lax.rsqrt(total * (1.0 / width) + 1e-06)
        recip[at, :] = r
        for k, block in enumerate(blocks):
            lanes = pl.ds(pl.multiple_of((m ^ k) * cols, cols), cols)
            normed[at, lanes] = (block[at, :].astype(F32) * r * gain[:, lanes]).astype(BF)
        return carry

    lax.fori_loop(0, rows // tile, step, 0)
    if near:
        quarter = rows // 2
        feats = cols // 2
        at = pl.ds(pl.multiple_of((m & 1) * quarter, quarter), quarter)
        for kz, send in enumerate(sends):
            for kx in range(2):
                block = lax.rem(z + kz, 4) * 2 + (x ^ kx)
                send[kx] = normed[at, pl.ds(pl.multiple_of(block * feats, feats), feats)]


def diagonal(f_quarter, flen):
    rows = lax.broadcasted_iota(jnp.int32, (f_quarter, f_quarter * flen), 0)
    lanes = lax.broadcasted_iota(jnp.int32, (f_quarter, f_quarter * flen), 1)
    return rows == lanes // flen


def fold(which, lanes, flen):
    rows = lax.broadcasted_iota(jnp.int32, (lanes, 128), 0)
    to = lax.broadcasted_iota(jnp.int32, (lanes, 128), 1)
    return jnp.where(to == lax.rem(rows, flen) + which * flen, 1.0, 0.0).astype(BF)


def forward_kernel(flen, idx, near, far, w_query, w_key, w_value, kmask, lmask,
                   early, probs, raw, upro, last, mixed):
    m = idx[0]
    half = 2 * (m >> 1)
    cols = w_key.shape[1]
    heads = cols // HEAD
    rows = near.shape[0] // 2
    fq = rows // flen
    scale = 1.0 / HEAD**0.5
    diag = diagonal(fq, flen)

    def quarter(i):
        return (near, far)[i // 2].at[pl.ds((i % 2) * rows, rows), :]

    for i in range(4):
        select = jnp.where(diag, lmask[i ^ half], 0.0).astype(BF)
        last[pl.ds(i * fq, fq), :] = dot(select, quarter(i)[...]).astype(BF)
    query = dot(last[...], w_query[...]).astype(BF)
    for h in range(heads):
        at = slice(h * HEAD, (h + 1) * HEAD)
        up = rdot(query[:, at], w_key[:, at]).astype(BF)
        for i in range(4):
            upro[i, pl.ds(h * fq, fq), :] = up[i * fq:(i + 1) * fq, :]
    for i in range(4):
        a = i ^ half
        to = pl.ds(pl.multiple_of(a * fq, fq), fq)
        normed = quarter(i)[...]
        score = rdot(upro[i], normed)
        mask = jnp.concatenate([jnp.where(diag, kmask[a], 0.0)] * heads, axis=0) > 0.0
        expo = jnp.where(mask, jnp.exp(score * scale), 0.0)
        prob = expo / jnp.sum(expo, axis=1, keepdims=True)
        raw[i] = score
        probs[i] = prob
        prob_b = prob.astype(BF)
        mix = dot(prob_b, normed).astype(BF)
        select = jnp.where(diag, lmask[a], 0.0).astype(BF)
        coef = dot(select, fold(2 * heads, rows, flen))
        for h in range(heads):
            mixed[h, pl.ds(i * fq, fq), :] = mix[h * fq:(h + 1) * fq, :]
            coef = coef + dot(prob_b[h * fq:(h + 1) * fq, :], fold(h, rows, flen))
        early[to, 0:cols] = query[i * fq:(i + 1) * fq, :]
        early[to, 2 * cols:2 * cols + 128] = coef.astype(BF)
    for h in range(heads):
        at = slice(h * HEAD, (h + 1) * HEAD)
        attended = dot(mixed[h], w_value[:, at]).astype(BF)
        for i in range(4):
            to = pl.ds(pl.multiple_of((i ^ half) * fq, fq), fq)
            early[to, cols + h * HEAD:cols + (h + 1) * HEAD] = attended[i * fq:(i + 1) * fq, :]


def backward_kernel(flen, idx, near, far, w_query, w_key, w_value, w_out, lmask,
                    g0, g1, g2, g3, early, probs, raw, upro,
                    late, product, d0, d1, d2, d3, tpro, vpro, mixed, dscore):
    m = idx[0]
    half = 2 * (m >> 1)
    cols = w_key.shape[1]
    heads = cols // HEAD
    rows = near.shape[0] // 2
    fq = rows // flen
    scale = 1.0 / HEAD**0.5
    diag = diagonal(fq, flen)

    def quarter(i):
        return (near, far)[i // 2].at[pl.ds((i % 2) * rows, rows), :]

    def here(i):
        return pl.ds(pl.multiple_of((i ^ half) * fq, fq), fq)

    d_att = jnp.zeros((4 * fq, cols), F32)
    for k, block in enumerate((g0, g1, g2, g3)):
        lanes = pl.ds(pl.multiple_of((m ^ k) * cols, cols), cols)
        grads = jnp.concatenate([block[here(i), :] for i in range(4)], axis=0)
        d_att = d_att + rdot(grads, w_out[:, lanes])
    d_att = d_att.astype(BF)
    for i in range(4):
        late[here(i), 0:cols] = d_att[i * fq:(i + 1) * fq, :]
    for h in range(heads):
        at = slice(h * HEAD, (h + 1) * HEAD)
        up = rdot(d_att[:, at], w_value[:, at]).astype(BF)
        for i in range(4):
            tpro[i, pl.ds(h * fq, fq), :] = up[i * fq:(i + 1) * fq, :]
    prods = []
    for i in range(4):
        normed = quarter(i)[...]
        d_prob = rdot(tpro[i], normed)
        prob = probs[i]
        d_score = prob * (d_prob - jnp.sum(prob * d_prob, axis=1, keepdims=True)) * scale
        score_b = d_score.astype(BF)
        prob_b = prob.astype(BF)
        dscore[i] = score_b
        prods.append(jnp.sum(d_score * raw[i] + prob_b.astype(F32) * d_prob, axis=0, keepdims=True))
        mix = dot(score_b, normed).astype(BF)
        coef = jnp.zeros((fq, 128), F32)
        for h in range(heads):
            mixed[h, pl.ds(i * fq, fq), :] = mix[h * fq:(h + 1) * fq, :]
            coef = coef + dot(score_b[h * fq:(h + 1) * fq, :], fold(heads + h, rows, flen))
        late[here(i), 2 * cols:2 * cols + 128] = coef.astype(BF)
    parts = []
    for h in range(heads):
        at = slice(h * HEAD, (h + 1) * HEAD)
        parts.append(dot(mixed[h], w_key[:, at]))
    d_query = jnp.concatenate(parts, axis=1).astype(BF)
    vpro[...] = rdot(d_query, w_query[...]).astype(BF)
    for i in range(4):
        dq = d_query[i * fq:(i + 1) * fq, :]
        late[here(i), cols:2 * cols] = dq
        query = early[here(i), 0:cols]
        inner = jnp.sum(query.astype(F32) * dq.astype(F32), axis=1, keepdims=True)
        select = jnp.where(diag, lmask[i ^ half], 0.0)
        product[pl.ds(i ^ half, 1), :] = prods[i] + jnp.sum(select * inner, axis=0, keepdims=True)
        to = pl.ds(pl.multiple_of((i ^ half) * rows, rows), rows)
        prob_b = probs[i].astype(BF)
        select = select.astype(BF)
        for k, out in enumerate((d0, d1, d2, d3)):
            lanes = pl.ds(pl.multiple_of((m ^ k) * cols, cols), cols)
            total = tdot(dscore[i], upro[i, :, lanes]) + tdot(prob_b, tpro[i, :, lanes])
            total = total + tdot(select, vpro[pl.ds(i * fq, fq), lanes])
            out[to, :] = total.astype(BF)


def weights_kernel(flen, n_src, idx, b0, b1, b2, b3, f0, f1, f2, f3, *refs):
    early, late = refs[:n_src], refs[n_src:2 * n_src]
    query_grad, key_grad, value_grad, out_grad = refs[2 * n_src:2 * n_src + 4]
    z_all, q_all, a_all, da_all, dq_all = refs[2 * n_src + 4:]
    m = idx[0]
    rows, feats = b0.shape[1:]
    fq = rows // flen
    cols = key_grad.shape[1]
    heads = cols // HEAD
    parts = 2 * heads + 1
    diag = jnp.where(diagonal(fq, flen), 1.0, 0.0)
    spread = jnp.concatenate([fold(p, rows, flen).T for p in range(parts)], axis=1)
    for out in (query_grad, key_grad, value_grad, out_grad):
        out[...] = jnp.zeros_like(out)
    for k, (normed, grads) in enumerate(zip((b0, b1, b2, b3), (f0, f1, f2, f3))):
        at = pl.ds(pl.multiple_of((m ^ k) * fq, fq), fq)
        for s in range(n_src):
            to = pl.ds(s * fq, fq)
            coef = early[s][at, 2 * cols:2 * cols + 128] + late[s][at, 2 * cols:2 * cols + 128]
            wide = dot(coef, spread)
            left = jnp.concatenate(
                [(wide[:, p * rows:(p + 1) * rows] * diag).astype(BF) for p in range(parts)], axis=0
            )
            mix = dot(left, normed[s]).astype(BF)
            for p in range(parts):
                z_all[p, to, :] = mix[p * fq:(p + 1) * fq, :]
            q_all[to, :] = early[s][at, 0:cols]
            a_all[to, :] = early[s][at, cols:2 * cols]
            da_all[to, :] = late[s][at, 0:cols]
            dq_all[to, :] = late[s][at, cols:2 * cols]
        for h in range(heads):
            lanes = slice(h * HEAD, (h + 1) * HEAD)
            key_grad[:, lanes] += tdot(z_all[heads + h], q_all[:, lanes])
            value_grad[:, lanes] += tdot(z_all[h], da_all[:, lanes])
        query_grad[...] += tdot(z_all[2 * heads], dq_all[...])
        out_grad[...] += tdot(a_all[...], grads[...].reshape(n_src * fq, feats))


def on_device(tok_grad, occurrence, owned, token_ids, embeds, gain, w_query, w_key, w_value, w_out):
    n_tok = lax.axis_size("tok")
    n_out = n_tok // 2
    f_dev, flen = token_ids.shape
    width = gain.shape[0]
    cols = w_key.shape[1]
    rows = f_dev * flen
    feats = width // n_tok
    fq = f_dev // 4
    quarter = fq * flen
    m = lax.axis_index("mdl")
    t = lax.axis_index("tok")
    z, x = t // 2, t % 2
    idx = jnp.stack([m, z, x, t]).astype(jnp.int32)

    def flip(array, bit):
        return lax.ppermute(array, "mdl", [(i, i ^ bit) for i in range(4)])

    def swap(array):
        return lax.ppermute(array, "tok", [(i, i ^ 1) for i in range(n_tok)])

    def shift(array, k):
        pairs = [(i, (i + 2 * k) % n_tok) for i in range(n_tok)]
        return lax.ppermute(array, "tok", pairs)

    owned_col = owned.reshape(-1, 1)
    occ_row = occurrence.reshape(1, -1)
    give = partial_sums(idx, owned_col, occ_row, tok_grad, n_out, f_dev, True, BF)
    took = swap(give)
    keep = partial_sums(idx, owned_col, occ_row, tok_grad, n_out, f_dev, False, F32)

    flat = embeds.reshape(rows, cols)
    pair = m >> 1
    mine = lax.dynamic_slice_in_dim(flat, pair * (rows // 2), rows // 2, 0)
    others = lax.dynamic_slice_in_dim(flat, (1 - pair) * (rows // 2), rows // 2, 0)
    near2 = flip(others, 2)
    far2 = flip(mine, 2)
    near1, near3 = flip(mine, 1), flip(near2, 1)
    far1, far3 = flip(others, 1), flip(far2, 1)
    gain_row = gain.reshape(1, width)
    near, near_r, *sends = call(
        functools.partial(norm_kernel, True),
        (idx, mine, near1, near2, near3, gain_row),
        [((rows // 2, width), BF), ((rows // 2, 1), F32)] + [((2, quarter, feats), BF)] * n_out,
    )

    both = keep + took.astype(F32)
    both = both.reshape(n_out, f_dev, cols)
    total = both[0]
    for k in range(1, n_out):
        total = total + shift(both[k].astype(BF), k).astype(F32)
    grad0 = total.astype(BF)
    grad2 = flip(grad0, 2)
    grad1, grad3 = flip(grad0, 1), flip(grad2, 1)

    def route(pieces):
        came = [pieces[0]] + [shift(pieces[k], k) for k in range(1, n_out)]
        direct = jnp.stack([c[0] for c in came])
        crossed = swap(jnp.stack([c[1] for c in came]))
        whole = jnp.concatenate([direct, crossed])
        from2 = flip(whole, 2)
        return whole, flip(whole, 1), from2, flip(from2, 1)

    normed_all = route(sends)

    far, far_r = call(
        functools.partial(norm_kernel, False),
        (idx, others, far1, far2, far3, gain_row),
        [((rows // 2, width), BF), ((rows // 2, 1), F32)],
    )

    length = jnp.sum((token_ids != 0).astype(jnp.int32), axis=1)
    positions = jnp.arange(flen, dtype=jnp.int32)
    lastmask = (positions[None, :] == (length - 1)[:, None]).astype(F32)
    keymask = (positions[None, :] < length[:, None]).astype(F32)
    lmask = lastmask.reshape(4, 1, quarter)
    kmask = keymask.reshape(4, 1, quarter)

    heads = cols // HEAD
    early, probs, raw, upro = call(
        functools.partial(forward_kernel, flen),
        (idx, near, far, w_query, w_key, w_value, kmask, lmask),
        [
            ((f_dev, 2 * cols + 128), BF),
            ((4, heads * fq, quarter), F32),
            ((4, heads * fq, quarter), F32),
            ((4, heads * fq, width), BF),
        ],
        [pltpu.VMEM((f_dev, width), BF), pltpu.VMEM((heads, f_dev, width), BF)],
    )

    def gather(item):
        direct = [item] + [shift(item, k) for k in range(1, n_out)]
        return direct + [swap(d) for d in direct]

    early_all = gather(early)

    late, product, d0, d1, d2, d3 = call(
        functools.partial(backward_kernel, flen),
        (idx, near, far, w_query, w_key, w_value, w_out, lmask,
         grad0, grad1, grad2, grad3, early, probs, raw, upro),
        [((f_dev, 2 * cols + 128), BF), ((4, quarter), F32)] + [((rows, cols), BF)] * 4,
        [
            pltpu.VMEM((4, heads * fq, width), BF),
            pltpu.VMEM((f_dev, width), BF),
            pltpu.VMEM((heads, f_dev, width), BF),
            pltpu.VMEM((4, heads * fq, quarter), BF),
        ],
    )
    late_all = gather(late)

    grad_full = jnp.stack([grad0, grad1, grad2, grad3])
    grad_quarter = lax.dynamic_slice_in_dim(grad_full, m * fq, fq, 1)
    pieces = []
    for k in range(n_out):
        block = lax.dynamic_index_in_dim(grad_quarter, m ^ lax.rem(z + k, n_out), 0, False)
        block = block.reshape(fq, 2, feats)
        first = lax.dynamic_index_in_dim(block, x, 1, False)
        second = lax.dynamic_index_in_dim(block, 1 - x, 1, False)
        pieces.append(jnp.stack([first, second]))
    grads_all = route(pieces)

    query_grad, key_grad, value_grad, out_grad = call(
        functools.partial(weights_kernel, flen, n_tok),
        (idx, *normed_all, *grads_all, *early_all, *late_all),
        [((feats, cols), F32)] * 3 + [((cols, feats), F32)],
        [
            pltpu.VMEM((2 * heads + 1, n_tok * fq, feats), BF),
            pltpu.VMEM((n_tok * fq, cols), BF),
            pltpu.VMEM((n_tok * fq, cols), BF),
            pltpu.VMEM((n_tok * fq, cols), BF),
            pltpu.VMEM((n_tok * fq, cols), BF),
        ],
    )

    product = product + flip(product, 1)
    product = product + flip(product, 2)
    own = d0.astype(F32) + flip(d1, 1).astype(F32)
    across = d2.astype(F32) + flip(d3, 1).astype(F32)
    summed = own + flip(across.astype(BF), 2).astype(F32)
    recip = jnp.where(
        pair == 0, jnp.concatenate([near_r, far_r]), jnp.concatenate([far_r, near_r])
    ).reshape(f_dev, flen, 1)
    gain_mine = lax.dynamic_slice_in_dim(gain, m * cols, cols, 0)
    scaled = summed.reshape(f_dev, flen, cols) * gain_mine
    weight = recip * recip * (product.reshape(f_dev, flen, 1) * (1.0 / width))
    result = recip * scaled - embeds.astype(F32) * weight
    result = result + jnp.where(lastmask[..., None] > 0, grad0.astype(F32)[:, None, :], 0.0)
    return (result.astype(BF), query_grad, key_grad, value_grad, out_grad)


def general(tok_grad, occurrence, owned, token_ids, embeds, gain, w_query, w_key, w_value, w_out):
    f32 = F32
    bf16 = BF
    n_tok = lax.axis_size("tok")
    fgrams = owned.shape[0]
    f_dev = fgrams // n_tok
    width = gain.shape[0]
    cols = w_key.shape[1]
    local_heads = cols // HEAD
    flen = token_ids.shape[1]
    scale = 1.0 / HEAD**0.5
    onehot = (owned[:, None] == occurrence[None, :]).astype(bf16)
    partial_sum = jnp.dot(onehot, tok_grad, preferred_element_type=f32)
    blocks = partial_sum.reshape(n_tok, f_dev, tok_grad.shape[1])
    arrived = lax.all_to_all(blocks, "tok", split_axis=0, concat_axis=0, tiled=True)
    fgram_sum = jnp.sum(arrived, axis=0)
    fgram_grad = fgram_sum.astype(bf16)
    full_grad = lax.all_gather(fgram_grad, "mdl", axis=1, tiled=True)
    whole_embeds = lax.all_gather(embeds, "mdl", axis=2, tiled=True)
    length = jnp.sum((token_ids != 0).astype(jnp.int32), axis=1)
    positions = jnp.arange(flen, dtype=jnp.int32)
    lastmask = positions[None, :] == (length - 1)[:, None]
    keymask = (positions[None, :] < length[:, None]).astype(f32)
    xfull = whole_embeds.astype(f32)
    recip = lax.rsqrt(jnp.mean(xfull * xfull, axis=-1) + 1e-06)
    normed = (xfull * recip[..., None] * gain).astype(bf16)
    normed_last = jnp.sum(jnp.where(lastmask[..., None], normed.astype(f32), 0.0), axis=1).astype(bf16)
    rows = normed.reshape(f_dev * flen, width)
    keys = dot(rows, w_key).astype(bf16).reshape(f_dev, flen, local_heads, HEAD)
    values = dot(rows, w_value).astype(bf16).reshape(f_dev, flen, local_heads, HEAD)
    query = dot(normed_last, w_query).astype(bf16).reshape(f_dev, local_heads, HEAD)
    keys32 = keys.astype(f32)
    values32 = values.astype(f32)
    query32 = query.astype(f32)
    scores = jnp.einsum("fhd,fjhd->fhj", query, keys, preferred_element_type=f32) * scale
    expo = jnp.exp(scores) * keymask[:, None, :]
    probs = expo / jnp.sum(expo, axis=-1, keepdims=True)
    probs_b = probs.astype(bf16)
    attended = jnp.einsum("fhj,fjhd->fhd", probs_b, values, preferred_element_type=f32)
    attended = attended.astype(bf16).reshape(f_dev, cols)
    d_att = rdot(full_grad, w_out).reshape(f_dev, local_heads, HEAD)
    d_prob = jnp.einsum("fhd,fjhd->fhj", d_att, values32)
    d_score = probs * (d_prob - jnp.sum(probs * d_prob, axis=-1, keepdims=True)) * scale
    d_query = jnp.einsum("fhj,fjhd->fhd", d_score, keys32).astype(bf16).reshape(f_dev, cols)
    d_key = jnp.einsum("fhj,fhd->fjhd", d_score, query32).astype(bf16).reshape(f_dev * flen, cols)
    d_value = jnp.einsum("fhj,fhd->fjhd", probs_b.astype(f32), d_att)
    d_value = d_value.astype(bf16).reshape(f_dev * flen, cols)
    d_normed = (rdot(d_key, w_key) + rdot(d_value, w_value)).reshape(f_dev, flen, width)
    from_query = rdot(d_query, w_query)
    d_normed = d_normed + jnp.where(lastmask[..., None], from_query[:, None, :], 0.0)
    feat_start = lax.axis_index("mdl") * embeds.shape[2]
    summed = lax.psum(d_normed, "mdl")
    scaled = summed * gain
    product = jnp.mean(xfull * scaled, axis=-1)
    result = recip[..., None] * scaled - xfull * (recip**3 * product)[..., None]
    result = lax.dynamic_slice_in_dim(result, feat_start, embeds.shape[2], 2)
    result = result + jnp.where(lastmask[..., None], fgram_grad.astype(f32)[:, None, :], 0.0)
    query_grad, key_grad, value_grad = (
        lax.psum_scatter(part, "tok", scatter_dimension=0, tiled=True)
        for part in (tdot(normed_last, d_query), tdot(rows, d_key), tdot(rows, d_value))
    )
    out_grad = lax.psum_scatter(tdot(attended, full_grad), "tok", scatter_dimension=1, tiled=True)
    return (result.astype(bf16), query_grad, key_grad, value_grad, out_grad)


def chosen(*args):
    fits = lax.axis_size("tok") == 8 and lax.axis_size("mdl") == 4
    return (on_device if fits else general)(*args)


def solution(mesh):
    return jax.shard_map(
        chosen,
        mesh=mesh,
        in_specs=(
            P("tok", "mdl"),
            P("tok"),
            P(),
            P("tok", None),
            P("tok", None, "mdl"),
            P(),
            P(None, "mdl"),
            P(None, "mdl"),
            P(None, "mdl"),
            P("mdl", None),
        ),
        out_specs=(
            P("tok", None, "mdl"),
            P("tok", "mdl"),
            P("tok", "mdl"),
            P("tok", "mdl"),
            P("mdl", "tok"),
        ),
        check_vma=False,
    )
```

```python
import functools

import jax
import jax.numpy as jnp
from jax import lax
from jax.experimental import pallas as pl
from jax.experimental.pallas import tpu as pltpu
from jax.sharding import PartitionSpec as P

HEAD = 128
BF = jnp.bfloat16
F32 = jnp.float32
VMEM = pl.BlockSpec(memory_space=pltpu.VMEM)
SMEM = pl.BlockSpec(memory_space=pltpu.SMEM)
LIMIT = 56 * 2**20
SCALE = 1.15e9


def dot(left, right):
    return jnp.dot(left, right, preferred_element_type=F32)


def tdot(left, right):
    return lax.dot_general(left, right, (((0,), (0,)), ((), ())), preferred_element_type=F32)


def rdot(left, right):
    return lax.dot_general(left, right, (((1,), (1,)), ((), ())), preferred_element_type=F32)


class Later:
    def __init__(self, copy, ref):
        self.copy, self.ref = copy, ref

    def get(self):
        if self.copy is not None:
            self.copy.wait()
            self.copy = None
        return self.ref


def get(ref):
    return ref.get() if isinstance(ref, Later) else ref


def call(body, ins, outs, micros, scratch=(), later=()):
    n_in, n_out, n_later = len(ins), len(outs), len(later)

    def kernel(*refs):
        given = list(refs[:n_in])
        rest = refs[n_in + n_out:]
        for j, i in enumerate(later):
            copy = pltpu.make_async_copy(given[i], rest[j], rest[n_later].at[j])
            copy.start()
            given[i] = Later(copy, rest[j])
        body(*given, *refs[n_in:n_in + n_out], *rest[n_later + (n_later > 0):])
        for j, i in enumerate(later):
            given[i].get()

    specs = [VMEM] * n_in
    specs[0] = SMEM
    for i in later:
        specs[i] = pl.BlockSpec(memory_space=pl.ANY)
    buffers = [pltpu.VMEM(ins[i].shape, ins[i].dtype) for i in later]
    if later:
        buffers.append(pltpu.SemaphoreType.DMA((n_later,)))
    return pl.pallas_call(
        kernel,
        in_specs=specs,
        out_specs=[VMEM] * len(outs),
        out_shape=[jax.ShapeDtypeStruct(s, t) for s, t in outs],
        scratch_shapes=[*buffers, *scratch],
        compiler_params=pltpu.CompilerParams(vmem_limit_bytes=LIMIT),
        cost_estimate=pl.CostEstimate(
            flops=int(micros * SCALE), bytes_accessed=0, transcendentals=0
        ),
    )(*ins)


def sums_kernel(n_out, other, idx, owned, occ, grads, out):
    z, x = idx[1], idx[2]
    f_dev = out.shape[0] // n_out
    side = 1 - x if other else x
    at = [pl.ds(pl.multiple_of(((z ^ k) * 2 + side) * f_dev, f_dev), f_dev) for k in range(n_out)]
    owners = jnp.concatenate([owned[a, :] for a in at], axis=0)
    onehot = jnp.where(owners == occ[...], 1.0, 0.0).astype(BF)
    out[...] = dot(onehot, get(grads)[...]).astype(out.dtype)


def norm_kernel(idx, x0, x1, x2, x3, gain, normed, recip, *sends):
    m, z, step = idx[0], idx[1], pl.program_id(0)
    tile, cols = x0.shape
    width = 4 * cols
    blocks = [block[...].astype(F32) for block in (x0, x1, x2, x3)]
    total = sum(jnp.sum(block * block, axis=1, keepdims=True) for block in blocks)
    r = lax.rsqrt(total * (1.0 / width) + 1e-06)
    recip[...] = r
    for k, block in enumerate(blocks):
        lanes = pl.ds(pl.multiple_of((m ^ k) * cols, cols), cols)
        normed[:, lanes] = (block * r * gain[:, lanes]).astype(BF)
    per = sends[0].shape[0] // tile

    @pl.when(step // per == m)
    def _():
        at = pl.ds(pl.multiple_of(lax.rem(step, per) * tile, tile), tile)
        for k, send in enumerate(sends):
            send[at, :] = normed[:, pl.ds(pl.multiple_of((z ^ k) * cols, cols), cols)]


def normalize(idx, blocks, gain, n_out):
    rows, cols = blocks[0].shape
    width = 4 * cols
    tile = 128
    quarter = rows // 4
    return pl.pallas_call(
        norm_kernel,
        grid_spec=pltpu.PrefetchScalarGridSpec(
            num_scalar_prefetch=1,
            grid=(rows // tile,),
            in_specs=[pl.BlockSpec((tile, cols), lambda i, idx: (i, 0))] * 4
            + [pl.BlockSpec((1, width), lambda i, idx: (0, 0))],
            out_specs=[
                pl.BlockSpec((tile, width), lambda i, idx: (i, 0)),
                pl.BlockSpec((tile, 1), lambda i, idx: (i, 0)),
            ]
            + [pl.BlockSpec((quarter, cols), lambda i, idx: (0, 0))] * n_out,
        ),
        out_shape=[
            jax.ShapeDtypeStruct((rows, width), BF),
            jax.ShapeDtypeStruct((rows, 1), F32),
        ]
        + [jax.ShapeDtypeStruct((quarter, cols), BF)] * n_out,
        compiler_params=pltpu.CompilerParams(vmem_limit_bytes=LIMIT),
        cost_estimate=pl.CostEstimate(flops=int(5 * SCALE), bytes_accessed=0, transcendentals=0),
    )(idx, *blocks, gain)


def diagonal(f_quarter, flen):
    rows = lax.broadcasted_iota(jnp.int32, (f_quarter, f_quarter * flen), 0)
    lanes = lax.broadcasted_iota(jnp.int32, (f_quarter, f_quarter * flen), 1)
    return rows == lanes // flen


def fold(which, lanes, flen):
    rows = lax.broadcasted_iota(jnp.int32, (lanes, 128), 0)
    to = lax.broadcasted_iota(jnp.int32, (lanes, 128), 1)
    return jnp.where(to == lax.rem(rows, flen) + which * flen, 1.0, 0.0).astype(BF)


def forward_kernel(flen, idx, normed, w_query, w_key, w_value, kmask, lmask,
                   early, probs, raw, upro, last, mixed):
    cols = w_query.ref.shape[1]
    heads = cols // HEAD
    normed = get(normed)
    rows = normed.shape[0] // 4
    fq = rows // flen
    scale = 1.0 / HEAD**0.5
    diag = diagonal(fq, flen)
    some = [slice(i * fq, (i + 1) * fq) for i in range(4)]

    for i in range(4):
        select = jnp.where(diag, lmask[i], 0.0).astype(BF)
        last[some[i], :] = dot(select, normed[i * rows:(i + 1) * rows, :]).astype(BF)
    query = dot(last[...], get(w_query)[...]).astype(BF)
    early[:, 0:cols] = query
    w_key = get(w_key)
    for h in range(heads):
        at = slice(h * HEAD, (h + 1) * HEAD)
        up = rdot(query[:, at], w_key[:, at]).astype(BF)
        for i in range(4):
            upro[i, some[h], :] = up[some[i], :]
    for i in range(4):
        part = normed[i * rows:(i + 1) * rows, :]
        score = rdot(upro[i], part)
        mask = jnp.concatenate([jnp.where(diag, kmask[i], 0.0)] * heads, axis=0) > 0.0
        expo = jnp.where(mask, jnp.exp(score * scale), 0.0)
        prob = expo / jnp.sum(expo, axis=1, keepdims=True)
        raw[i] = score
        probs[i] = prob
        prob_b = prob.astype(BF)
        mix = dot(prob_b, part).astype(BF)
        select = jnp.where(diag, lmask[i], 0.0).astype(BF)
        coef = dot(select, fold(2 * heads, rows, flen))
        for h in range(heads):
            mixed[h, some[i], :] = mix[some[h], :]
            coef = coef + dot(prob_b[some[h], :], fold(h, rows, flen))
        early[some[i], 2 * cols:2 * cols + 128] = coef.astype(BF)
    w_value = get(w_value)
    for h in range(heads):
        at = slice(h * HEAD, (h + 1) * HEAD)
        early[:, cols + h * HEAD:cols + (h + 1) * HEAD] = dot(mixed[h], w_value[:, at]).astype(BF)


def scores_kernel(flen, idx, normed, w_key, w_value, w_out, lmask, g0, g1, g2, g3, early, probs, raw,
                  late, product, tpro, dscore, probs_b, mixed):
    m = idx[0]
    cols = w_key.ref.shape[1]
    heads = cols // HEAD
    rows = normed.ref.shape[0] // 4
    fq = rows // flen
    scale = 1.0 / HEAD**0.5
    diag = diagonal(fq, flen)
    some = [slice(i * fq, (i + 1) * fq) for i in range(4)]

    d_att = jnp.zeros((4 * fq, cols), F32)
    w_out = get(w_out)
    for k, block in enumerate((g0, g1, g2, g3)):
        lanes = pl.ds(pl.multiple_of((m ^ k) * cols, cols), cols)
        d_att = d_att + rdot(block[...], w_out[:, lanes])
    d_att = d_att.astype(BF)
    late[:, 0:cols] = d_att
    w_value = get(w_value)
    for h in range(heads):
        at = slice(h * HEAD, (h + 1) * HEAD)
        up = rdot(d_att[:, at], w_value[:, at]).astype(BF)
        for i in range(4):
            tpro[i, some[h], :] = up[some[i], :]
    prods = []
    normed = get(normed)
    for i in range(4):
        part = normed[i * rows:(i + 1) * rows, :]
        d_prob = rdot(tpro[i], part)
        prob = get(probs)[i]
        d_score = prob * (d_prob - jnp.sum(prob * d_prob, axis=1, keepdims=True)) * scale
        score_b = d_score.astype(BF)
        prob_b = prob.astype(BF)
        dscore[i] = score_b
        probs_b[i] = prob_b
        inner = d_score * get(raw)[i] + prob_b.astype(F32) * d_prob
        prods.append(jnp.sum(inner, axis=0, keepdims=True))
        mix = dot(score_b, part).astype(BF)
        coef = jnp.zeros((fq, 128), F32)
        for h in range(heads):
            mixed[h, some[i], :] = mix[some[h], :]
            coef = coef + dot(score_b[some[h], :], fold(heads + h, rows, flen))
        late[some[i], 2 * cols:2 * cols + 128] = coef.astype(BF)
    parts = []
    w_key = get(w_key)
    for h in range(heads):
        at = slice(h * HEAD, (h + 1) * HEAD)
        parts.append(dot(mixed[h], w_key[:, at]))
    d_query = jnp.concatenate(parts, axis=1).astype(BF)
    late[:, cols:2 * cols] = d_query
    inner = early[:, 0:cols].astype(F32) * d_query.astype(F32)
    inner = jnp.sum(inner, axis=1, keepdims=True)
    for i in range(4):
        select = jnp.where(diag, lmask[i], 0.0)
        product[i:i + 1, :] = prods[i] + jnp.sum(select * inner[some[i], :], axis=0, keepdims=True)


def normed_kernel(flen, idx, w_query, lmask, late, upro, tpro, dscore, probs_b, d0, d1, d2, d3, vpro):
    m = idx[0]
    rows = dscore.shape[2]
    fq = rows // flen
    cols = d0.shape[1]
    diag = diagonal(fq, flen)
    vpro[...] = rdot(late[:, cols:2 * cols], get(w_query)[...]).astype(BF)
    upro, tpro = get(upro), get(tpro)
    for i in range(4):
        select = jnp.where(diag, lmask[i], 0.0).astype(BF)
        left = jnp.concatenate([dscore[i], probs_b[i], select], axis=0)
        for k, out in enumerate((d0, d1, d2, d3)):
            lanes = pl.ds(pl.multiple_of((m ^ k) * cols, cols), cols)
            right = jnp.concatenate(
                [upro[i, :, lanes], tpro[i, :, lanes], vpro[i * fq:(i + 1) * fq, lanes]], axis=0
            )
            out[i * rows:(i + 1) * rows, :] = tdot(left, right).astype(BF)


def out_kernel(idx, g0, g1, g2, g3, e0, e1, e2, e3, mine, other, att):
    m, z, x = idx[0], idx[1], idx[2]
    cols = mine.shape[0]
    half = mine.shape[1]
    for s, early in enumerate((e0, e1, e2, e3)):
        att[s] = get(early)[:, cols:2 * cols]
    for k, grads in enumerate((g0, g1, g2, g3)):
        left = att[(z ^ m) ^ k]
        own = tdot(left, grads[:, pl.ds(pl.multiple_of(x * half, half), half)])
        far = tdot(left, grads[:, pl.ds(pl.multiple_of((1 - x) * half, half), half)])
        mine[...] = own if k == 0 else mine[...] + own
        total = far if k == 0 else total + far
    other[...] = total.astype(BF)


def mix_rows(coef, normed, parts, flen):
    rows = normed.shape[0]
    fq = rows // flen
    diag = jnp.where(diagonal(fq, flen), 1.0, 0.0)
    spread = jnp.concatenate([fold(p, rows, flen).T for p in parts], axis=1)
    wide = dot(coef, spread)
    left = [(wide[:, j * rows:(j + 1) * rows] * diag).astype(BF) for j in range(len(parts))]
    return dot(jnp.concatenate(left, axis=0), normed).astype(BF)


def value_kernel(flen, heads, idx, b0, b1, b2, b3, *refs):
    early, late = refs[:4], refs[4:8]
    mine, other, z_all, d_all = refs[8:]
    m, x = idx[0], idx[2]
    rows = b0.ref.shape[1]
    fq = rows // flen
    cols = mine.shape[1]
    half = mine.shape[0]
    for k, normed in enumerate((b0, b1, b2, b3)):
        at = pl.ds(pl.multiple_of((m ^ k) * fq, fq), fq)
        for s in range(4):
            to = slice((k * 4 + s) * fq, (k * 4 + s + 1) * fq)
            coef = get(early[s])[at, 2 * cols:2 * cols + 128]
            mix = mix_rows(coef, get(normed)[s], range(heads), flen)
            for p in range(heads):
                z_all[p, to, :] = mix[p * fq:(p + 1) * fq, :]
            d_all[to, :] = get(late[s])[at, 0:cols]
    for h in range(heads):
        lanes = slice(h * HEAD, (h + 1) * HEAD)
        own = pl.ds(pl.multiple_of(x * half, half), half)
        far = pl.ds(pl.multiple_of((1 - x) * half, half), half)
        mine[:, lanes] = tdot(z_all[h, :, own], d_all[:, lanes])
        other[:, lanes] = tdot(z_all[h, :, far], d_all[:, lanes]).astype(BF)


def key_kernel(flen, heads, idx, b0, b1, b2, b3, *refs):
    early, late = refs[:4], refs[4:8]
    key_mine, query_mine, other, z_all, q_all, d_all = refs[8:]
    m, x = idx[0], idx[2]
    rows = b0.ref.shape[1]
    fq = rows // flen
    cols = key_mine.shape[1]
    half = key_mine.shape[0]
    for k, normed in enumerate((b0, b1, b2, b3)):
        at = pl.ds(pl.multiple_of((m ^ k) * fq, fq), fq)
        for s in range(4):
            to = slice((k * 4 + s) * fq, (k * 4 + s + 1) * fq)
            first, second = get(early[s]), get(late[s])
            coef = first[at, 2 * cols:2 * cols + 128] + second[at, 2 * cols:2 * cols + 128]
            mix = mix_rows(coef, get(normed)[s], range(heads, 2 * heads + 1), flen)
            for p in range(heads + 1):
                z_all[p, to, :] = mix[p * fq:(p + 1) * fq, :]
            q_all[to, :] = first[at, 0:cols]
            d_all[to, :] = second[at, cols:2 * cols]
    own = pl.ds(pl.multiple_of(x * half, half), half)
    far = pl.ds(pl.multiple_of((1 - x) * half, half), half)
    for h in range(heads):
        lanes = slice(h * HEAD, (h + 1) * HEAD)
        key_mine[:, lanes] = tdot(z_all[h, :, own], q_all[:, lanes])
        other[0, :, lanes] = tdot(z_all[h, :, far], q_all[:, lanes]).astype(BF)
    query_mine[...] = tdot(z_all[heads, :, own], d_all[...])
    other[1] = tdot(z_all[heads, :, far], d_all[...]).astype(BF)


def on_device(tok_grad, occurrence, owned, token_ids, embeds, gain, w_query, w_key, w_value, w_out):
    n_tok = lax.axis_size("tok")
    n_out = n_tok // 2
    f_dev, flen = token_ids.shape
    width = gain.shape[0]
    cols = w_key.shape[1]
    rows = f_dev * flen
    feats = width // n_tok
    fq = f_dev // 4
    quarter = fq * flen
    heads = cols // HEAD
    m = lax.axis_index("mdl")
    t = lax.axis_index("tok")
    z, x = t // 2, t % 2
    idx = jnp.stack([m, z, x, t]).astype(jnp.int32)

    def flip(array, bit):
        return lax.ppermute(array, "mdl", [(i, i ^ bit) for i in range(4)])

    def swap(array):
        return lax.ppermute(array, "tok", [(i, i ^ 1) for i in range(n_tok)])

    def cross(array, k):
        return lax.ppermute(array, "tok", [(i, i ^ (2 * k)) for i in range(n_tok)])

    flat = embeds.reshape(rows, cols)
    flat2 = flip(flat, 2)

    owned_col = owned.reshape(-1, 1)
    occ_row = occurrence.reshape(1, -1)

    def sums(other, dtype):
        return call(
            functools.partial(sums_kernel, n_out, other),
            (idx, owned_col, occ_row, tok_grad),
            [((n_out * f_dev, cols), dtype)],
            4,
            later=(3,),
        )[0]

    took = swap(sums(True, BF))
    keep = sums(False, F32)
    flat1 = flip(flat, 1)
    both = (keep + took.astype(F32)).reshape(n_out, f_dev, cols)
    total = both[0]
    for k in range(1, n_out):
        total = total + cross(both[k].astype(BF), k).astype(F32)
    flat3 = flip(flat2, 1)
    gain_row = gain.reshape(1, width)
    normed, recip, *sends = normalize(idx, (flat, flat1, flat2, flat3), gain_row, n_out)
    grad0 = total.astype(BF)
    grad2 = flip(grad0, 2)
    grad1, grad3 = flip(grad0, 1), flip(grad2, 1)

    def share(whole):
        from2 = flip(whole, 2)
        return whole, flip(whole, 1), from2, flip(from2, 1)

    length = jnp.sum((token_ids != 0).astype(jnp.int32), axis=1)
    positions = jnp.arange(flen, dtype=jnp.int32)
    lastmask = (positions[None, :] == (length - 1)[:, None]).astype(F32)
    keymask = (positions[None, :] < length[:, None]).astype(F32)
    lmask = lastmask.reshape(4, 1, quarter)
    kmask = keymask.reshape(4, 1, quarter)

    normed_all = share(jnp.stack([sends[0]] + [cross(sends[k], k) for k in range(1, n_out)]))

    item = ((f_dev, 2 * cols + 128), BF)
    square = (4, heads * fq, quarter)
    tall = ((4, heads * fq, width), BF)
    early, probs, raw, upro = call(
        functools.partial(forward_kernel, flen),
        (idx, normed, w_query, w_key, w_value, kmask, lmask),
        [item, (square, F32), (square, F32), tall],
        11,
        [pltpu.VMEM((f_dev, width), BF), pltpu.VMEM((heads, f_dev, width), BF)],
        later=(1, 2, 3, 4),
    )

    def gather(own):
        one, two = cross(own, 1), cross(own, 2)
        return [own, one, two, cross(two, 1)]

    early_all = gather(early)

    pairs = []
    for a in range(n_out):
        for b in range(2):
            for c in range(4):
                pairs.append(((a * 2 + b) * 4 + c, (c * 2 + b) * 4 + a))
    grads_all = share(lax.ppermute(grad0, ("tok", "mdl"), pairs))

    late, product, tpro, dscore, probs_b = call(
        functools.partial(scores_kernel, flen),
        (idx, normed, w_key, w_value, w_out, lmask, grad0, grad1, grad2, grad3, early, probs, raw),
        [item, ((4, quarter), F32), tall, (square, BF), (square, BF)],
        10,
        [pltpu.VMEM((heads, f_dev, width), BF)],
        later=(4, 3, 1, 11, 12, 2),
    )
    late_all = gather(late)
    d0, d1, d2, d3 = call(
        functools.partial(normed_kernel, flen),
        (idx, w_query, lmask, late, upro, tpro, dscore, probs_b),
        [((rows, cols), BF)] * 4,
        8,
        [pltpu.VMEM((f_dev, width), BF)],
        later=(1, 4, 5),
    )

    out_mine, out_other = call(
        out_kernel,
        (idx, *grads_all, *early_all),
        [((cols, feats), F32), ((cols, feats), BF)],
        3,
        [pltpu.VMEM((4, f_dev, cols), BF)],
        later=(5, 6, 7, 8),
    )
    out_grad = out_mine + swap(out_other).astype(F32)
    f_all = n_out * f_dev
    value_mine, value_other = call(
        functools.partial(value_kernel, flen, heads),
        (idx, *normed_all, *early_all, *late_all),
        [((feats, cols), F32), ((feats, cols), BF)],
        5,
        [pltpu.VMEM((heads, f_all, 2 * feats), BF), pltpu.VMEM((f_all, cols), BF)],
        later=(5, 6, 7, 8, 9, 10, 11, 12, 1, 2, 3, 4),
    )
    value_grad = value_mine + swap(value_other).astype(F32)
    key_mine, query_mine, both_other = call(
        functools.partial(key_kernel, flen, heads),
        (idx, *normed_all, *early_all, *late_all),
        [((feats, cols), F32), ((feats, cols), F32), ((2, feats, cols), BF)],
        6,
        [
            pltpu.VMEM((heads + 1, f_all, 2 * feats), BF),
            pltpu.VMEM((f_all, cols), BF),
            pltpu.VMEM((f_all, cols), BF),
        ],
        later=(5, 6, 7, 8, 9, 10, 11, 12, 1, 2, 3, 4),
    )
    crossed = swap(both_other)
    key_grad = key_mine + crossed[0].astype(F32)
    query_grad = query_mine + crossed[1].astype(F32)

    product = product + flip(product, 1)
    product = product + flip(product, 2)
    own = d0.astype(F32) + flip(d1, 1).astype(F32)
    across = d2.astype(F32) + flip(d3, 1).astype(F32)
    summed = own + flip(across.astype(BF), 2).astype(F32)
    gain_mine = lax.dynamic_slice_in_dim(gain, m * cols, cols, 0)
    scaled = summed.reshape(f_dev, flen, cols) * gain_mine
    recip = recip.reshape(f_dev, flen, 1)
    weight = recip * recip * (product.reshape(f_dev, flen, 1) * (1.0 / width))
    result = recip * scaled - embeds.astype(F32) * weight
    result = result + jnp.where(lastmask[..., None] > 0, grad0.astype(F32)[:, None, :], 0.0)
    return (result.astype(BF), query_grad, key_grad, value_grad, out_grad)


def general(tok_grad, occurrence, owned, token_ids, embeds, gain, w_query, w_key, w_value, w_out):
    f32 = F32
    bf16 = BF
    n_tok = lax.axis_size("tok")
    fgrams = owned.shape[0]
    f_dev = fgrams // n_tok
    width = gain.shape[0]
    cols = w_key.shape[1]
    local_heads = cols // HEAD
    flen = token_ids.shape[1]
    scale = 1.0 / HEAD**0.5
    onehot = (owned[:, None] == occurrence[None, :]).astype(bf16)
    partial_sum = jnp.dot(onehot, tok_grad, preferred_element_type=f32)
    blocks = partial_sum.reshape(n_tok, f_dev, tok_grad.shape[1])
    arrived = lax.all_to_all(blocks, "tok", split_axis=0, concat_axis=0, tiled=True)
    fgram_sum = jnp.sum(arrived, axis=0)
    fgram_grad = fgram_sum.astype(bf16)
    full_grad = lax.all_gather(fgram_grad, "mdl", axis=1, tiled=True)
    whole_embeds = lax.all_gather(embeds, "mdl", axis=2, tiled=True)
    length = jnp.sum((token_ids != 0).astype(jnp.int32), axis=1)
    positions = jnp.arange(flen, dtype=jnp.int32)
    lastmask = positions[None, :] == (length - 1)[:, None]
    keymask = (positions[None, :] < length[:, None]).astype(f32)
    xfull = whole_embeds.astype(f32)
    recip = lax.rsqrt(jnp.mean(xfull * xfull, axis=-1) + 1e-06)
    normed = (xfull * recip[..., None] * gain).astype(bf16)
    normed_last = jnp.sum(jnp.where(lastmask[..., None], normed.astype(f32), 0.0), axis=1).astype(bf16)
    rows = normed.reshape(f_dev * flen, width)
    keys = dot(rows, w_key).astype(bf16).reshape(f_dev, flen, local_heads, HEAD)
    values = dot(rows, w_value).astype(bf16).reshape(f_dev, flen, local_heads, HEAD)
    query = dot(normed_last, w_query).astype(bf16).reshape(f_dev, local_heads, HEAD)
    keys32 = keys.astype(f32)
    values32 = values.astype(f32)
    query32 = query.astype(f32)
    scores = jnp.einsum("fhd,fjhd->fhj", query, keys, preferred_element_type=f32) * scale
    expo = jnp.exp(scores) * keymask[:, None, :]
    probs = expo / jnp.sum(expo, axis=-1, keepdims=True)
    probs_b = probs.astype(bf16)
    attended = jnp.einsum("fhj,fjhd->fhd", probs_b, values, preferred_element_type=f32)
    attended = attended.astype(bf16).reshape(f_dev, cols)
    d_att = rdot(full_grad, w_out).reshape(f_dev, local_heads, HEAD)
    d_prob = jnp.einsum("fhd,fjhd->fhj", d_att, values32)
    d_score = probs * (d_prob - jnp.sum(probs * d_prob, axis=-1, keepdims=True)) * scale
    d_query = jnp.einsum("fhj,fjhd->fhd", d_score, keys32).astype(bf16).reshape(f_dev, cols)
    d_key = jnp.einsum("fhj,fhd->fjhd", d_score, query32).astype(bf16).reshape(f_dev * flen, cols)
    d_value = jnp.einsum("fhj,fhd->fjhd", probs_b.astype(f32), d_att)
    d_value = d_value.astype(bf16).reshape(f_dev * flen, cols)
    d_normed = (rdot(d_key, w_key) + rdot(d_value, w_value)).reshape(f_dev, flen, width)
    from_query = rdot(d_query, w_query)
    d_normed = d_normed + jnp.where(lastmask[..., None], from_query[:, None, :], 0.0)
    feat_start = lax.axis_index("mdl") * embeds.shape[2]
    summed = lax.psum(d_normed, "mdl")
    scaled = summed * gain
    product = jnp.mean(xfull * scaled, axis=-1)
    result = recip[..., None] * scaled - xfull * (recip**3 * product)[..., None]
    result = lax.dynamic_slice_in_dim(result, feat_start, embeds.shape[2], 2)
    result = result + jnp.where(lastmask[..., None], fgram_grad.astype(f32)[:, None, :], 0.0)
    query_grad, key_grad, value_grad = (
        lax.psum_scatter(part, "tok", scatter_dimension=0, tiled=True)
        for part in (tdot(normed_last, d_query), tdot(rows, d_key), tdot(rows, d_value))
    )
    out_grad = lax.psum_scatter(tdot(attended, full_grad), "tok", scatter_dimension=1, tiled=True)
    return (result.astype(bf16), query_grad, key_grad, value_grad, out_grad)


def chosen(*args):
    fits = lax.axis_size("tok") == 8 and lax.axis_size("mdl") == 4
    return (on_device if fits else general)(*args)


def solution(mesh):
    return jax.shard_map(
        chosen,
        mesh=mesh,
        in_specs=(
            P("tok", "mdl"),
            P("tok"),
            P(),
            P("tok", None),
            P("tok", None, "mdl"),
            P(),
            P(None, "mdl"),
            P(None, "mdl"),
            P(None, "mdl"),
            P("mdl", None),
        ),
        out_specs=(
            P("tok", None, "mdl"),
            P("tok", "mdl"),
            P("tok", "mdl"),
            P("tok", "mdl"),
            P("mdl", "tok"),
        ),
        check_vma=False,
    )
```

```python
import functools

import jax
import jax.numpy as jnp
from jax import lax
from jax.experimental import pallas as pl
from jax.experimental.pallas import tpu as pltpu
from jax.sharding import PartitionSpec as P

HEAD = 128
BF = jnp.bfloat16
F32 = jnp.float32
VMEM = pl.BlockSpec(memory_space=pltpu.VMEM)
SMEM = pl.BlockSpec(memory_space=pltpu.SMEM)
LIMIT = 56 * 2**20
SCALE = 1.15e9
COSTS = [0.1, 0.1, 0.1, 5, 0.1, 0.1, 5, 0.1, 0.1]
TIES = [1, 2, 1, 0, 2, 1, 0, 0, 1, 1, 1, 1, 0, 0, 1, 1, 0, 0, 0, 0, 1, 1, 1, 0]


def dot(left, right):
    return jnp.dot(left, right, preferred_element_type=F32)


def tdot(left, right):
    return lax.dot_general(left, right, (((0,), (0,)), ((), ())), preferred_element_type=F32)


def rdot(left, right):
    return lax.dot_general(left, right, (((1,), (1,)), ((), ())), preferred_element_type=F32)


def after(array, *others, when=True):
    return lax.optimization_barrier((array, *others))[0] if when else array


class Later:
    def __init__(self, copy, ref):
        self.copy, self.ref = copy, ref

    def get(self):
        if self.copy is not None:
            self.copy.wait()
            self.copy = None
        return self.ref


def get(ref):
    return ref.get() if isinstance(ref, Later) else ref


class Sooner:
    def __init__(self, copy, ref):
        self.copy, self.ref, self.started = copy, ref, False

    def start(self):
        self.copy.start()
        self.started = True


def call(body, ins, outs, micros, scratch=(), later=(), sooner=()):
    n_in, n_out, n_later, n_sooner = len(ins), len(outs), len(later), len(sooner)

    def kernel(*refs):
        given = list(refs[:n_in])
        made = list(refs[n_in:n_in + n_out])
        rest = refs[n_in + n_out:]
        buffers, rest = rest[:n_later + n_sooner], rest[n_later + n_sooner:]
        if buffers:
            sems, rest = rest[0], rest[1:]
        for j, i in enumerate(later):
            copy = pltpu.make_async_copy(given[i], buffers[j], sems.at[j])
            copy.start()
            given[i] = Later(copy, buffers[j])
        for j, i in enumerate(sooner):
            buffer = buffers[n_later + j]
            made[i] = Sooner(pltpu.make_async_copy(buffer, made[i], sems.at[n_later + j]), buffer)
        body(*given, *made, *rest)
        for i in later:
            given[i].get()
        for i in sooner:
            if not made[i].started:
                made[i].start()
        for i in sooner:
            made[i].copy.wait()

    in_specs, out_specs = [VMEM] * n_in, [VMEM] * n_out
    in_specs[0] = SMEM
    for i in later:
        in_specs[i] = pl.BlockSpec(memory_space=pl.ANY)
    for i in sooner:
        out_specs[i] = pl.BlockSpec(memory_space=pl.ANY)
    buffers = [pltpu.VMEM(ins[i].shape, ins[i].dtype) for i in later]
    buffers += [pltpu.VMEM(*outs[i]) for i in sooner]
    if buffers:
        buffers.append(pltpu.SemaphoreType.DMA((n_later + n_sooner,)))
    return pl.pallas_call(
        kernel,
        in_specs=in_specs,
        out_specs=out_specs,
        out_shape=[jax.ShapeDtypeStruct(s, t) for s, t in outs],
        scratch_shapes=[*buffers, *scratch],
        compiler_params=pltpu.CompilerParams(vmem_limit_bytes=LIMIT),
        cost_estimate=pl.CostEstimate(
            flops=int(micros * SCALE), bytes_accessed=0, transcendentals=0
        ),
    )(*ins)


def sums_kernel(n_out, other, idx, owned, occ, grads, out):
    z, x = idx[1], idx[2]
    f_dev = out.shape[0] // n_out
    side = 1 - x if other else x
    at = [pl.ds(pl.multiple_of(((z ^ k) * 2 + side) * f_dev, f_dev), f_dev) for k in range(n_out)]
    owners = jnp.concatenate([owned[a, :] for a in at], axis=0)
    onehot = jnp.where(owners == occ[...], 1.0, 0.0).astype(BF)
    out[...] = dot(onehot, get(grads)[...]).astype(out.dtype)


def norm_rows(m, tile, sources, gain, normed, recip):
    rows, cols = sources[0].shape
    width = 4 * cols

    def step(i, carry):
        at = pl.ds(pl.multiple_of(i * tile, tile), tile)
        total = jnp.zeros((tile, 1), F32)
        for block in sources:
            part = block[at, :].astype(F32)
            total = total + jnp.sum(part * part, axis=1, keepdims=True)
        r = lax.rsqrt(total * (1.0 / width) + 1e-06)
        if recip is not None:
            recip[at, :] = r
        for k, block in enumerate(sources):
            lanes = pl.ds(pl.multiple_of((m ^ k) * cols, cols), cols)
            normed[at, lanes] = (block[at, :].astype(F32) * r * gain[:, lanes]).astype(BF)
        return carry

    lax.fori_loop(0, rows // tile, step, 0, unroll=True)


def quarter_kernel(idx, x0, x1, x2, x3, gain, *refs):
    sends, normed = refs[:-1], refs[-1]
    m, z = idx[0], idx[1]
    cols = x0.shape[1]
    norm_rows(m, 32, (x0, x1, x2, x3), gain, normed, None)
    for k, send in enumerate(sends):
        send[...] = normed[:, pl.ds(pl.multiple_of((z ^ k) * cols, cols), cols)]


def norm_quarter(idx, blocks, gain):
    rows, cols = blocks[0].shape
    width = 4 * cols
    quarter = rows // 4
    return pl.pallas_call(
        quarter_kernel,
        grid_spec=pltpu.PrefetchScalarGridSpec(
            num_scalar_prefetch=1,
            grid=(1,),
            in_specs=[pl.BlockSpec((quarter, cols), lambda i, idx: (idx[0], 0))] * 4
            + [pl.BlockSpec((1, width), lambda i, idx: (0, 0))],
            out_specs=[pl.BlockSpec((quarter, cols), lambda i, idx: (0, 0))] * 4,
            scratch_shapes=[pltpu.VMEM((quarter, width), BF)],
        ),
        out_shape=[jax.ShapeDtypeStruct((quarter, cols), BF)] * 4,
        compiler_params=pltpu.CompilerParams(vmem_limit_bytes=LIMIT),
        cost_estimate=pl.CostEstimate(flops=int(COSTS[1] * SCALE), bytes_accessed=0, transcendentals=0),
    )(idx, *blocks, gain)


def diagonal(f_quarter, flen):
    rows = lax.broadcasted_iota(jnp.int32, (f_quarter, f_quarter * flen), 0)
    lanes = lax.broadcasted_iota(jnp.int32, (f_quarter, f_quarter * flen), 1)
    return rows == lanes // flen


def fold(which, lanes, flen):
    rows = lax.broadcasted_iota(jnp.int32, (lanes, 128), 0)
    to = lax.broadcasted_iota(jnp.int32, (lanes, 128), 1)
    return jnp.where(to == lax.rem(rows, flen) + which * flen, 1.0, 0.0).astype(BF)


def fold_heads(values, heads, fq, flen, shift):
    lanes = lax.broadcasted_iota(jnp.int32, (heads * fq, 128), 1)
    rows = lax.broadcasted_iota(jnp.int32, (heads * fq, 128), 0)
    back = lax.broadcasted_iota(jnp.int32, (fq * flen, 128), 0)
    to = lax.broadcasted_iota(jnp.int32, (fq * flen, 128), 1)
    every = jnp.where(lax.rem(back, flen) == lax.rem(to, flen), 1.0, 0.0).astype(BF)
    wide = jnp.where(lanes // flen == rows // fq + shift, dot(values, every), 0.0)
    total = wide[0:fq]
    for h in range(1, heads):
        total = total + wide[h * fq:(h + 1) * fq]
    return total


def forward_kernel(flen, idx, x0, x1, x2, x3, gain, w_query, w_key, w_value, kmask, lmask,
                   early, probs, raw, upro, normed_out, recip, last, mixed):
    m = idx[0]
    cols = w_query.ref.shape[1]
    heads = cols // HEAD
    normed = normed_out.ref
    rows = normed.shape[0] // 4
    fq = rows // flen
    scale = 1.0 / HEAD**0.5
    diag = diagonal(fq, flen)
    some = [slice(i * fq, (i + 1) * fq) for i in range(4)]

    norm_rows(m, 32, [get(x) for x in (x0, x1, x2, x3)], gain, normed, recip)
    normed_out.start()
    selects = [jnp.where(diag, lmask[i], 0.0).astype(BF) for i in range(4)]
    for i in range(4):
        last[some[i], :] = dot(selects[i], normed[i * rows:(i + 1) * rows, :]).astype(BF)
    query = dot(last[...], get(w_query)[...]).astype(BF)
    early[:, 0:cols] = query
    w_key = get(w_key)
    for h in range(heads):
        at = slice(h * HEAD, (h + 1) * HEAD)
        up = rdot(query[:, at], w_key[:, at]).astype(BF)
        for i in range(4):
            upro.ref[i, some[h], :] = up[some[i], :]
    upro.start()
    for i in range(4):
        part = normed[i * rows:(i + 1) * rows, :]
        score = rdot(upro.ref[i], part)
        mask = jnp.concatenate([jnp.where(diag, kmask[i], 0.0)] * heads, axis=0) > 0.0
        expo = jnp.where(mask, jnp.exp(score * scale), 0.0)
        prob = expo / jnp.sum(expo, axis=1, keepdims=True)
        raw[i] = score
        probs[i] = prob
        prob_b = prob.astype(BF)
        mix = dot(prob_b, part).astype(BF)
        for h in range(heads):
            mixed[h, some[i], :] = mix[some[h], :]
        coef = fold_heads(prob_b, heads, fq, flen, 0) + fold_heads(selects[i], 1, fq, flen, 2 * heads)
        early[some[i], 2 * cols:2 * cols + 128] = coef.astype(BF)
    w_value = get(w_value)
    for h in range(heads):
        at = slice(h * HEAD, (h + 1) * HEAD)
        early[:, cols + h * HEAD:cols + (h + 1) * HEAD] = dot(mixed[h], w_value[:, at]).astype(BF)


def in_turn(m, ref, cols):
    return jnp.concatenate(
        [ref[:, pl.ds(pl.multiple_of((m ^ k) * cols, cols), cols)] for k in range(4)], axis=1
    )


def scores_kernel(flen, idx, normed, w_key, w_value, w_out, lmask, g0, g1, g23, early, probs, raw,
                  late, product, tpro, dscore, probs_b, mixed):
    m = idx[0]
    cols = w_key.ref.shape[1]
    heads = cols // HEAD
    rows = normed.ref.shape[0] // 4
    fq = rows // flen
    scale = 1.0 / HEAD**0.5
    diag = diagonal(fq, flen)
    some = [slice(i * fq, (i + 1) * fq) for i in range(4)]

    grads = jnp.concatenate([g[...] for g in (g0, g1, g23.at[0], g23.at[1])], axis=1)
    d_att = rdot(grads, in_turn(m, get(w_out), cols)).astype(BF)
    late[:, 0:cols] = d_att
    w_value = get(w_value)
    for h in range(heads):
        at = slice(h * HEAD, (h + 1) * HEAD)
        up = rdot(d_att[:, at], w_value[:, at]).astype(BF)
        for i in range(4):
            tpro.ref[i, some[h], :] = up[some[i], :]
    tpro.start()
    prods = []
    normed = get(normed)
    for i in range(4):
        part = normed[i * rows:(i + 1) * rows, :]
        d_prob = rdot(tpro.ref[i], part)
        prob = get(probs)[i]
        d_score = prob * (d_prob - jnp.sum(prob * d_prob, axis=1, keepdims=True)) * scale
        score_b = d_score.astype(BF)
        prob_b = prob.astype(BF)
        dscore[i] = score_b
        probs_b[i] = prob_b
        inner = d_score * get(raw)[i] + prob_b.astype(F32) * d_prob
        prods.append(jnp.sum(inner, axis=0, keepdims=True))
        mix = dot(score_b, part).astype(BF)
        for h in range(heads):
            mixed[h, some[i], :] = mix[some[h], :]
        coef = fold_heads(score_b, heads, fq, flen, heads)
        late[some[i], 2 * cols:2 * cols + 128] = coef.astype(BF)
    parts = []
    w_key = get(w_key)
    for h in range(heads):
        at = slice(h * HEAD, (h + 1) * HEAD)
        parts.append(dot(mixed[h], w_key[:, at]))
    d_query = jnp.concatenate(parts, axis=1).astype(BF)
    late[:, cols:2 * cols] = d_query
    inner = early[:, 0:cols].astype(F32) * d_query.astype(F32)
    inner = jnp.sum(inner, axis=1, keepdims=True)
    for i in range(4):
        select = jnp.where(diag, lmask[i], 0.0)
        product[i:i + 1, :] = prods[i] + jnp.sum(select * inner[some[i], :], axis=0, keepdims=True)


def normed_kernel(flen, idx, w_query, lmask, late, product, upro, tpro, dscore, probs_b, d0, d2, d1, d3, vpro):
    m = idx[0]
    rows = dscore.shape[2]
    fq = rows // flen
    cols = d0.shape[1]
    diag = diagonal(fq, flen)
    vpro[...] = rdot(late[:, cols:2 * cols], get(w_query)[...]).astype(BF)
    upro, tpro = get(upro), get(tpro)
    for i in range(4):
        select = jnp.where(diag, lmask[i], 0.0).astype(BF)
        left = jnp.concatenate([dscore[i], probs_b[i], select], axis=0)
        right = jnp.concatenate(
            [in_turn(m, upro.at[i], cols), in_turn(m, tpro.at[i], cols),
             in_turn(m, vpro.at[pl.ds(i * fq, fq), :], cols)], axis=0
        )
        total = tdot(left, right).astype(BF)
        for k, out in enumerate((d0, d1, d2, d3)):
            out[i * rows:(i + 1) * rows, :] = total[:, k * cols:(k + 1) * cols]
    for out in (d0, d1, d2, d3):
        out[4 * rows:4 * rows + 16, :] = jnp.zeros((16, cols), BF)
    for out in (d2, d3):
        out[4 * rows:4 * rows + 16, 0:rows] = jnp.concatenate(
            [product[...], jnp.zeros((12, rows), F32)], axis=0
        ).astype(BF)


def mix_rows(parts, flen, coefs, normed, z_all):
    fq = z_all.shape[1] // 16
    rows = fq * flen
    diag = jnp.where(diagonal(fq, flen), 1.0, 0.0)
    spread = jnp.concatenate([fold(p, rows, flen).T for p in parts], axis=1)
    for k, block in enumerate(normed):
        block = get(block)
        wide = dot(coefs[k], spread)
        for s in range(4):
            left = jnp.concatenate(
                [(wide[s * fq:(s + 1) * fq, j * rows:(j + 1) * rows] * diag).astype(BF)
                 for j in range(len(parts))], axis=0
            )
            mix = dot(left, block[s * rows:(s + 1) * rows, :]).astype(BF)
            for j in range(len(parts)):
                z_all[j, (k * 4 + s) * fq:(k * 4 + s + 1) * fq, :] = mix[j * fq:(j + 1) * fq, :]


def first_kernel(flen, heads, idx, b0, b1, b2, b3, e0, e1, e2, e3,
                 out_mine, out_other, z_value, z_last, z_all, att, all_grads):
    m, z, x = idx[0], idx[1], idx[2]
    early = (e0, e1, e2, e3)
    cols, half = out_mine.shape
    f_dev = e0.ref.shape[0]
    fq = f_dev // 4
    own = pl.ds(pl.multiple_of(x * half, half), half)
    far = pl.ds(pl.multiple_of((1 - x) * half, half), half)
    at = [pl.ds(pl.multiple_of((m ^ k) * fq, fq), fq) for k in range(4)]
    last = slice(2 * cols, 2 * cols + 128)
    coefs = [jnp.concatenate([get(e)[a, last] for e in early], axis=0) for a in at]
    mix_rows((*range(heads), 2 * heads), flen, coefs, (b0, b1, b2, b3), z_all)
    z_value.ref[...] = z_all[0:heads]
    z_last.ref[...] = z_all[heads]
    z_value.start()
    z_last.start()
    for k, rows in enumerate((b0, b1, b2, b3)):
        to = pl.ds(pl.multiple_of(((z ^ m) ^ k) * f_dev, f_dev), f_dev)
        all_grads[to, :] = get(rows)[4 * fq * flen:4 * fq * flen + f_dev, :]
    for s in range(4):
        att[s * f_dev:(s + 1) * f_dev, :] = get(early[s])[:, cols:2 * cols]
    out_mine[...] = tdot(att[...], all_grads[:, own])
    out_other[...] = tdot(att[...], all_grads[:, far]).astype(BF)


def value_kernel(heads, idx, z_value, z_last, l0, l1, l2, l3, value_mine, query_mine, other, d_all, dq_all):
    m, x = idx[0], idx[2]
    half, cols = value_mine.shape
    fq = l0.shape[0] // 4
    for k in range(4):
        a = pl.ds(pl.multiple_of((m ^ k) * fq, fq), fq)
        for s, late in enumerate((l0, l1, l2, l3)):
            to = slice((k * 4 + s) * fq, (k * 4 + s + 1) * fq)
            d_all[to, :] = late[a, 0:cols]
            dq_all[to, :] = late[a, cols:2 * cols]
    own = pl.ds(pl.multiple_of(x * half, half), half)
    far = pl.ds(pl.multiple_of((1 - x) * half, half), half)
    z_value, z_last = get(z_value), get(z_last)
    for h in range(heads):
        lanes = slice(h * HEAD, (h + 1) * HEAD)
        value_mine[:, lanes] = tdot(z_value[h, :, own], d_all[:, lanes])
        other[0, :, lanes] = tdot(z_value[h, :, far], d_all[:, lanes]).astype(BF)
    query_mine[...] = tdot(z_last[:, own], dq_all[...])
    other[1] = tdot(z_last[:, far], dq_all[...]).astype(BF)


def key_kernel(flen, heads, idx, b0, b1, b2, b3, *refs):
    early, late, refs = refs[:4], refs[4:8], refs[8:]
    mine, other, z_all, q_all = refs
    m, x = idx[0], idx[2]
    half, cols = mine.shape
    fq = late[0].ref.shape[0] // 4
    at = [pl.ds(pl.multiple_of((m ^ k) * fq, fq), fq) for k in range(4)]
    last = slice(2 * cols, 2 * cols + 128)
    coefs = [jnp.concatenate([get(item)[a, last] for item in late], axis=0) for a in at]
    mix_rows(range(heads, 2 * heads), flen, coefs, (b0, b1, b2, b3), z_all)
    for k, a in enumerate(at):
        for s in range(4):
            q_all[(k * 4 + s) * fq:(k * 4 + s + 1) * fq, :] = get(early[s])[a, 0:cols]
    own = pl.ds(pl.multiple_of(x * half, half), half)
    far = pl.ds(pl.multiple_of((1 - x) * half, half), half)
    for h in range(heads):
        lanes = slice(h * HEAD, (h + 1) * HEAD)
        mine[:, lanes] = tdot(z_all[h, :, own], q_all[:, lanes])
        other[:, lanes] = tdot(z_all[h, :, far], q_all[:, lanes]).astype(BF)


def on_device(tok_grad, occurrence, owned, token_ids, embeds, gain, w_query, w_key, w_value, w_out):
    n_tok = lax.axis_size("tok")
    n_out = n_tok // 2
    f_dev, flen = token_ids.shape
    width = gain.shape[0]
    cols = w_key.shape[1]
    rows = f_dev * flen
    feats = width // n_tok
    fq = f_dev // 4
    quarter = fq * flen
    heads = cols // HEAD
    m = lax.axis_index("mdl")
    t = lax.axis_index("tok")
    z, x = t // 2, t % 2
    idx = jnp.stack([m, z, x, t]).astype(jnp.int32)

    def flip(array, bit):
        return lax.ppermute(array, "mdl", [(i, i ^ bit) for i in range(4)])

    def swap(array):
        return lax.ppermute(array, "tok", [(i, i ^ 1) for i in range(n_tok)])

    def cross(array, k):
        return lax.ppermute(array, "tok", [(i, i ^ (2 * k)) for i in range(n_tok)])

    flat = embeds.reshape(rows, cols)
    flat2 = flip(flat, 2)

    owned_col = owned.reshape(-1, 1)
    occ_row = occurrence.reshape(1, -1)

    def sums(other, dtype, owners):
        return call(
            functools.partial(sums_kernel, n_out, other),
            (idx, owners, occ_row, tok_grad),
            [((n_out * f_dev, cols), dtype)],
            COSTS[0],
            later=(3,),
        )[0]

    give = sums(True, BF, owned_col)
    took = swap(give)
    keep = sums(False, F32, owned_col)
    flat2 = after(flat2, keep, when=TIES[11])
    flat1 = flip(flat, 1)
    both = (keep + took.astype(F32)).reshape(n_out, f_dev, cols)
    pieces = [both[k].astype(BF) for k in range(1, n_out)]
    came = [cross(piece, k) for k, piece in enumerate(pieces, 1)]
    flat2 = after(flat2, *pieces, when=TIES[23])
    flat3 = flip(flat2, 1)
    gain_row = gain.reshape(1, width)

    length = jnp.sum((token_ids != 0).astype(jnp.int32), axis=1)
    positions = jnp.arange(flen, dtype=jnp.int32)
    lastmask = (positions[None, :] == (length - 1)[:, None]).astype(F32)
    keymask = (positions[None, :] < length[:, None]).astype(F32)
    lmask = lastmask.reshape(4, 1, quarter)
    kmask = keymask.reshape(4, 1, quarter)

    sends = norm_quarter(idx, (flat, flat1, flat2, flat3), gain_row)
    far_rows = [cross(sends[k], k) for k in range(1, n_out)]

    item = ((f_dev, 2 * cols + 128), BF)
    square = (4, heads * fq, quarter)
    tall = ((4, heads * fq, width), BF)
    def sums_over_tok(*before):
        total = both[0]
        for piece in came:
            total = total + after(piece, *before).astype(F32)
        grad0 = total.astype(BF)
        grad1 = flip(grad0, 1)
        return grad0, grad1, flip(jnp.stack([grad0, grad1]), 2)

    if not TIES[18]:
        grad0, grad1, grad23 = sums_over_tok(sends[0])
    early, probs, raw, upro, normed, recip = call(
        functools.partial(forward_kernel, flen),
        (idx, flat, flat1, flat2, flat3, (after(gain_row, (grad0, grad23)[TIES[1] - 1]) if TIES[1] else gain_row), w_query, w_key, w_value, kmask, lmask),
        [item, (square, F32), (square, F32), tall, ((rows, width), BF), ((rows, 1), F32)],
        COSTS[2],
        [pltpu.VMEM((f_dev, width), BF), pltpu.VMEM((heads, f_dev, width), BF)],
        later=(1, 2, 3, 4, 6, 7, 8),
        sooner=(3, 4),
    )
    if TIES[18]:
        grad0, grad1, grad23 = sums_over_tok(early)
    pairs = []
    for a in range(n_out):
        for b in range(2):
            for c in range(4):
                pairs.append(((a * 2 + b) * 4 + c, (c * 2 + b) * 4 + a))
    turned = lax.ppermute(after(after(grad0, early, when=TIES[16]), grad23, when=TIES[19] > 1), ("tok", "mdl"), pairs)
    far_rows = [after(r, early, when=TIES[2]) for r in far_rows]
    turned = after(turned, early, when=TIES[2])
    sent = after(early, grad23, when=TIES[19])
    early1, early2 = cross(sent, 1), cross(sent, 2)
    gate1 = after(lmask, *far_rows, when=TIES[12])
    if TIES[17]:
        gate1 = after(gate1, early1)

    late, product, tpro, dscore, probs_b = call(
        functools.partial(scores_kernel, flen),
        (idx, normed, w_key, w_value, w_out, gate1, grad0, grad1, grad23, early, probs, raw),
        [item, ((4, quarter), F32), tall, (square, BF), (square, BF)],
        COSTS[4],
        [pltpu.VMEM((heads, f_dev, width), BF)],
        later=(4, 3, 1, 10, 11, 2),
        sooner=(2,),
    )
    if TIES[20]:
        early1, early2 = after(early1, late), after(early2, late)
    early_all = (early, early1, early2, cross(early2, 1) if TIES[10] else cross(early, 3))
    sent = after(late, early1, early2, when=TIES[21])
    late1, late2 = cross(sent, 1), cross(sent, 2)
    gate = after(lmask, late1, when=TIES[4])
    gate = after(gate, late2, when=TIES[4] > 1)
    gate = after(gate, early1, early2, when=TIES[14])
    whole = jnp.concatenate([sends[0]] + far_rows + [turned])
    from2 = flip(after(whole, late, when=TIES[3]), 2)
    gate = after(gate, whole, when=TIES[15])
    d0, d2, d1, d3 = call(
        functools.partial(normed_kernel, flen),
        (idx, w_query, gate, late, product, upro, tpro, dscore, probs_b),
        [((rows + 16, cols), BF)] * 4,
        COSTS[5],
        [pltpu.VMEM((f_dev, width), BF)],
        later=(1, 5, 6),
    )
    beside = (flip(d1, 1), flip(d3, 1))
    from2 = after(from2, d0, when=TIES[6])
    normed_all = (whole, flip(whole, 1), from2, flip(from2, 1))
    across = (d2.astype(F32) + beside[1].astype(F32)).astype(BF)
    own = d0.astype(F32) + beside[0].astype(F32)

    late_all = (late, late1, late2, cross(after(late2, late1, when=TIES[5]), 1))


    f_all = n_out * f_dev
    out_mine, out_other, z_value, z_last = call(
        functools.partial(first_kernel, flen, heads),
        (after(idx, across, when=TIES[7]), *normed_all, *early_all),
        [((cols, feats), F32), ((cols, feats), BF), ((heads, f_all, 2 * feats), BF), ((f_all, 2 * feats), BF)],
        COSTS[6],
        [
            pltpu.VMEM((heads + 1, f_all, 2 * feats), BF),
            pltpu.VMEM((f_all, cols), BF),
            pltpu.VMEM((f_all, 2 * feats), BF),
        ],
        later=(5, 6, 7, 8, 1, 2, 3, 4),
        sooner=(2, 3),
    )
    out_grad = out_mine + swap(out_other).astype(F32)
    value_mine, query_mine, both_other = call(
        functools.partial(value_kernel, heads),
        (after(idx, out_grad, when=TIES[13]), z_value, z_last, *late_all),
        [((feats, cols), F32), ((feats, cols), F32), ((2, feats, cols), BF)],
        COSTS[7],
        [pltpu.VMEM((f_all, cols), BF), pltpu.VMEM((f_all, cols), BF)],
        later=(1, 2),
    )
    key_mine, key_other = call(
        functools.partial(key_kernel, flen, heads),
        (after(idx, both_other), *normed_all, *early_all, *late_all),
        [((feats, cols), F32), ((feats, cols), BF)],
        COSTS[8],
        [pltpu.VMEM((heads, f_all, 2 * feats), BF), pltpu.VMEM((f_all, cols), BF)],
        later=(9, 10, 11, 12, 1, 2, 3, 4, 5, 6, 7, 8),
    )
    came = after(swap(both_other), key_other, when=TIES[8])
    value_grad = value_mine + came[0].astype(F32)
    query_grad = query_mine + came[1].astype(F32)
    key_grad = key_mine + after(swap(key_other), value_grad, query_grad, out_grad, when=TIES[22]).astype(F32)

    crossed_over = after(flip(across, 2), key_other, when=TIES[9]).astype(F32)
    summed = own[0:rows] + crossed_over[0:rows]
    product = (across.astype(F32) + crossed_over)[rows:rows + 4, 0:quarter]
    gain_mine = lax.dynamic_slice_in_dim(gain, m * cols, cols, 0)
    scaled = summed.reshape(f_dev, flen, cols) * gain_mine
    recip = recip.reshape(f_dev, flen, 1)
    weight = recip * recip * (product.reshape(f_dev, flen, 1) * (1.0 / width))
    result = recip * scaled - embeds.astype(F32) * weight
    result = result + jnp.where(lastmask[..., None] > 0, grad0.astype(F32)[:, None, :], 0.0)
    return (result.astype(BF), query_grad, key_grad, value_grad, out_grad)


def general(tok_grad, occurrence, owned, token_ids, embeds, gain, w_query, w_key, w_value, w_out):
    f32 = F32
    bf16 = BF
    n_tok = lax.axis_size("tok")
    fgrams = owned.shape[0]
    f_dev = fgrams // n_tok
    width = gain.shape[0]
    cols = w_key.shape[1]
    local_heads = cols // HEAD
    flen = token_ids.shape[1]
    scale = 1.0 / HEAD**0.5
    onehot = (owned[:, None] == occurrence[None, :]).astype(bf16)
    partial_sum = jnp.dot(onehot, tok_grad, preferred_element_type=f32)
    blocks = partial_sum.reshape(n_tok, f_dev, tok_grad.shape[1])
    arrived = lax.all_to_all(blocks, "tok", split_axis=0, concat_axis=0, tiled=True)
    fgram_sum = jnp.sum(arrived, axis=0)
    fgram_grad = fgram_sum.astype(bf16)
    full_grad = lax.all_gather(fgram_grad, "mdl", axis=1, tiled=True)
    whole_embeds = lax.all_gather(embeds, "mdl", axis=2, tiled=True)
    length = jnp.sum((token_ids != 0).astype(jnp.int32), axis=1)
    positions = jnp.arange(flen, dtype=jnp.int32)
    lastmask = positions[None, :] == (length - 1)[:, None]
    keymask = (positions[None, :] < length[:, None]).astype(f32)
    xfull = whole_embeds.astype(f32)
    recip = lax.rsqrt(jnp.mean(xfull * xfull, axis=-1) + 1e-06)
    normed = (xfull * recip[..., None] * gain).astype(bf16)
    normed_last = jnp.sum(jnp.where(lastmask[..., None], normed.astype(f32), 0.0), axis=1).astype(bf16)
    rows = normed.reshape(f_dev * flen, width)
    keys = dot(rows, w_key).astype(bf16).reshape(f_dev, flen, local_heads, HEAD)
    values = dot(rows, w_value).astype(bf16).reshape(f_dev, flen, local_heads, HEAD)
    query = dot(normed_last, w_query).astype(bf16).reshape(f_dev, local_heads, HEAD)
    keys32 = keys.astype(f32)
    values32 = values.astype(f32)
    query32 = query.astype(f32)
    scores = jnp.einsum("fhd,fjhd->fhj", query, keys, preferred_element_type=f32) * scale
    expo = jnp.exp(scores) * keymask[:, None, :]
    probs = expo / jnp.sum(expo, axis=-1, keepdims=True)
    probs_b = probs.astype(bf16)
    attended = jnp.einsum("fhj,fjhd->fhd", probs_b, values, preferred_element_type=f32)
    attended = attended.astype(bf16).reshape(f_dev, cols)
    d_att = rdot(full_grad, w_out).reshape(f_dev, local_heads, HEAD)
    d_prob = jnp.einsum("fhd,fjhd->fhj", d_att, values32)
    d_score = probs * (d_prob - jnp.sum(probs * d_prob, axis=-1, keepdims=True)) * scale
    d_query = jnp.einsum("fhj,fjhd->fhd", d_score, keys32).astype(bf16).reshape(f_dev, cols)
    d_key = jnp.einsum("fhj,fhd->fjhd", d_score, query32).astype(bf16).reshape(f_dev * flen, cols)
    d_value = jnp.einsum("fhj,fhd->fjhd", probs_b.astype(f32), d_att)
    d_value = d_value.astype(bf16).reshape(f_dev * flen, cols)
    d_normed = (rdot(d_key, w_key) + rdot(d_value, w_value)).reshape(f_dev, flen, width)
    from_query = rdot(d_query, w_query)
    d_normed = d_normed + jnp.where(lastmask[..., None], from_query[:, None, :], 0.0)
    feat_start = lax.axis_index("mdl") * embeds.shape[2]
    summed = lax.psum(d_normed, "mdl")
    scaled = summed * gain
    product = jnp.mean(xfull * scaled, axis=-1)
    result = recip[..., None] * scaled - xfull * (recip**3 * product)[..., None]
    result = lax.dynamic_slice_in_dim(result, feat_start, embeds.shape[2], 2)
    result = result + jnp.where(lastmask[..., None], fgram_grad.astype(f32)[:, None, :], 0.0)
    query_grad, key_grad, value_grad = (
        lax.psum_scatter(part, "tok", scatter_dimension=0, tiled=True)
        for part in (tdot(normed_last, d_query), tdot(rows, d_key), tdot(rows, d_value))
    )
    out_grad = lax.psum_scatter(tdot(attended, full_grad), "tok", scatter_dimension=1, tiled=True)
    return (result.astype(bf16), query_grad, key_grad, value_grad, out_grad)


def chosen(*args):
    fits = lax.axis_size("tok") == 8 and lax.axis_size("mdl") == 4
    return (on_device if fits else general)(*args)


def solution(mesh):
    return jax.shard_map(
        chosen,
        mesh=mesh,
        in_specs=(
            P("tok", "mdl"),
            P("tok"),
            P(),
            P("tok", None),
            P("tok", None, "mdl"),
            P(),
            P(None, "mdl"),
            P(None, "mdl"),
            P(None, "mdl"),
            P("mdl", None),
        ),
        out_specs=(
            P("tok", None, "mdl"),
            P("tok", "mdl"),
            P("tok", "mdl"),
            P("tok", "mdl"),
            P("mdl", "tok"),
        ),
        check_vma=False,
    )
```

```python
import functools

import jax
import jax.numpy as jnp
from jax import lax
from jax.experimental import pallas as pl
from jax.experimental.pallas import tpu as pltpu
from jax.sharding import PartitionSpec as P

HEAD = 128
BF = jnp.bfloat16
F32 = jnp.float32
VMEM = pl.BlockSpec(memory_space=pltpu.VMEM)
SMEM = pl.BlockSpec(memory_space=pltpu.SMEM)
LIMIT = 56 * 2**20
SCALE = 1.15e9
COSTS = [0.1, 0.1, 0.1, 5, 0.1, 0.1, 5, 0.1, 0.1]
TIES = [1, 1, 1, 0, 1, 1, 0, 1, 1, 1, 1, 1, 0, 0, 1, 1, 0, 0, 0, 1, 0, 1, 1, 1]


def dot(left, right):
    return jnp.dot(left, right, preferred_element_type=F32)


def tdot(left, right):
    return lax.dot_general(left, right, (((0,), (0,)), ((), ())), preferred_element_type=F32)


def rdot(left, right):
    return lax.dot_general(left, right, (((1,), (1,)), ((), ())), preferred_element_type=F32)


def after(array, *others, when=True):
    return lax.optimization_barrier((array, *others))[0] if when else array


class Later:
    def __init__(self, copy, ref):
        self.copy, self.ref = copy, ref

    def get(self):
        if self.copy is not None:
            self.copy.wait()
            self.copy = None
        return self.ref


def get(ref):
    return ref.get() if isinstance(ref, Later) else ref


class Sooner:
    def __init__(self, copy, ref):
        self.copy, self.ref, self.started = copy, ref, False

    def start(self):
        self.copy.start()
        self.started = True


def call(body, ins, outs, micros, scratch=(), later=(), sooner=()):
    n_in, n_out, n_later, n_sooner = len(ins), len(outs), len(later), len(sooner)

    def kernel(*refs):
        given = list(refs[:n_in])
        made = list(refs[n_in:n_in + n_out])
        rest = refs[n_in + n_out:]
        buffers, rest = rest[:n_later + n_sooner], rest[n_later + n_sooner:]
        if buffers:
            sems, rest = rest[0], rest[1:]
        for j, i in enumerate(later):
            copy = pltpu.make_async_copy(given[i], buffers[j], sems.at[j])
            copy.start()
            given[i] = Later(copy, buffers[j])
        for j, i in enumerate(sooner):
            buffer = buffers[n_later + j]
            made[i] = Sooner(pltpu.make_async_copy(buffer, made[i], sems.at[n_later + j]), buffer)
        body(*given, *made, *rest)
        for i in later:
            given[i].get()
        for i in sooner:
            if not made[i].started:
                made[i].start()
        for i in sooner:
            made[i].copy.wait()

    in_specs, out_specs = [VMEM] * n_in, [VMEM] * n_out
    in_specs[0] = SMEM
    for i in later:
        in_specs[i] = pl.BlockSpec(memory_space=pl.ANY)
    for i in sooner:
        out_specs[i] = pl.BlockSpec(memory_space=pl.ANY)
    buffers = [pltpu.VMEM(ins[i].shape, ins[i].dtype) for i in later]
    buffers += [pltpu.VMEM(*outs[i]) for i in sooner]
    if buffers:
        buffers.append(pltpu.SemaphoreType.DMA((n_later + n_sooner,)))
    return pl.pallas_call(
        kernel,
        in_specs=in_specs,
        out_specs=out_specs,
        out_shape=[jax.ShapeDtypeStruct(s, t) for s, t in outs],
        scratch_shapes=[*buffers, *scratch],
        compiler_params=pltpu.CompilerParams(vmem_limit_bytes=LIMIT),
        cost_estimate=pl.CostEstimate(
            flops=int(micros * SCALE), bytes_accessed=0, transcendentals=0
        ),
    )(*ins)


def sums_kernel(n_out, other, idx, owned, occ, grads, out):
    z, x = idx[1], idx[2]
    f_dev = out.shape[0] // n_out
    side = 1 - x if other else x
    at = [pl.ds(pl.multiple_of(((z ^ k) * 2 + side) * f_dev, f_dev), f_dev) for k in range(n_out)]
    owners = jnp.concatenate([owned[a, :] for a in at], axis=0)
    onehot = jnp.where(owners == occ[...], 1.0, 0.0).astype(BF)
    out[...] = dot(onehot, get(grads)[...]).astype(out.dtype)


def add_kernel(idx, keep, took, own, *pieces):
    f_dev = own.shape[0]
    own[...] = keep[0:f_dev, :] + took[0:f_dev, :].astype(F32)
    for k, piece in enumerate(pieces, 1):
        at = slice(k * f_dev, (k + 1) * f_dev)
        piece[...] = (keep[at, :] + took[at, :].astype(F32)).astype(BF)


def norm_rows(m, tile, sources, gain, normed, recip):
    rows, cols = sources[0].shape
    width = 4 * cols

    def step(i, carry):
        at = pl.ds(pl.multiple_of(i * tile, tile), tile)
        total = jnp.zeros((tile, 1), F32)
        for block in sources:
            part = block[at, :].astype(F32)
            total = total + jnp.sum(part * part, axis=1, keepdims=True)
        r = lax.rsqrt(total * (1.0 / width) + 1e-06)
        if recip is not None:
            recip[at, :] = r
        for k, block in enumerate(sources):
            lanes = pl.ds(pl.multiple_of((m ^ k) * cols, cols), cols)
            normed[at, lanes] = (block[at, :].astype(F32) * r * gain[:, lanes]).astype(BF)
        return carry

    lax.fori_loop(0, rows // tile, step, 0, unroll=True)


def quarter_kernel(idx, x0, x1, x2, x3, gain, *refs):
    sends, normed = refs[:-1], refs[-1]
    m, z = idx[0], idx[1]
    cols = x0.shape[1]
    norm_rows(m, 32, (x0, x1, x2, x3), gain, normed, None)
    for k, send in enumerate(sends):
        send[...] = normed[:, pl.ds(pl.multiple_of((z ^ k) * cols, cols), cols)]


def norm_quarter(idx, blocks, gain):
    rows, cols = blocks[0].shape
    width = 4 * cols
    quarter = rows // 4
    return pl.pallas_call(
        quarter_kernel,
        grid_spec=pltpu.PrefetchScalarGridSpec(
            num_scalar_prefetch=1,
            grid=(1,),
            in_specs=[pl.BlockSpec((quarter, cols), lambda i, idx: (idx[0], 0))] * 4
            + [pl.BlockSpec((1, width), lambda i, idx: (0, 0))],
            out_specs=[pl.BlockSpec((quarter, cols), lambda i, idx: (0, 0))] * 4,
            scratch_shapes=[pltpu.VMEM((quarter, width), BF)],
        ),
        out_shape=[jax.ShapeDtypeStruct((quarter, cols), BF)] * 4,
        compiler_params=pltpu.CompilerParams(vmem_limit_bytes=LIMIT),
        cost_estimate=pl.CostEstimate(flops=int(COSTS[1] * SCALE), bytes_accessed=0, transcendentals=0),
    )(idx, *blocks, gain)


def diagonal(f_quarter, flen):
    rows = lax.broadcasted_iota(jnp.int32, (f_quarter, f_quarter * flen), 0)
    lanes = lax.broadcasted_iota(jnp.int32, (f_quarter, f_quarter * flen), 1)
    return rows == lanes // flen


def fold(which, lanes, flen):
    rows = lax.broadcasted_iota(jnp.int32, (lanes, 128), 0)
    to = lax.broadcasted_iota(jnp.int32, (lanes, 128), 1)
    return jnp.where(to == lax.rem(rows, flen) + which * flen, 1.0, 0.0).astype(BF)


def fold_heads(values, heads, fq, flen, shift):
    lanes = lax.broadcasted_iota(jnp.int32, (heads * fq, 128), 1)
    rows = lax.broadcasted_iota(jnp.int32, (heads * fq, 128), 0)
    back = lax.broadcasted_iota(jnp.int32, (fq * flen, 128), 0)
    to = lax.broadcasted_iota(jnp.int32, (fq * flen, 128), 1)
    every = jnp.where(lax.rem(back, flen) == lax.rem(to, flen), 1.0, 0.0).astype(BF)
    wide = jnp.where(lanes // flen == rows // fq + shift, dot(values, every), 0.0)
    total = wide[0:fq]
    for h in range(1, heads):
        total = total + wide[h * fq:(h + 1) * fq]
    return total


def forward_kernel(flen, idx, x0, x1, x2, x3, gain, w_query, w_key, w_value, kmask, lmask,
                   early, probs, raw, upro, normed_out, recip, last, mixed):
    m = idx[0]
    cols = w_query.ref.shape[1]
    heads = cols // HEAD
    normed = normed_out.ref
    rows = normed.shape[0] // 4
    fq = rows // flen
    scale = 1.0 / HEAD**0.5
    diag = diagonal(fq, flen)
    some = [slice(i * fq, (i + 1) * fq) for i in range(4)]

    norm_rows(m, 32, [get(x) for x in (x0, x1, x2, x3)], gain, normed, recip)
    normed_out.start()
    selects = [jnp.where(diag, lmask[i], 0.0).astype(BF) for i in range(4)]
    for i in range(4):
        last[some[i], :] = dot(selects[i], normed[i * rows:(i + 1) * rows, :]).astype(BF)
    query = dot(last[...], get(w_query)[...]).astype(BF)
    early[:, 0:cols] = query
    w_key = get(w_key)
    for h in range(heads):
        at = slice(h * HEAD, (h + 1) * HEAD)
        up = rdot(query[:, at], w_key[:, at]).astype(BF)
        for i in range(4):
            upro.ref[i, some[h], :] = up[some[i], :]
    upro.start()
    for i in range(4):
        part = normed[i * rows:(i + 1) * rows, :]
        score = rdot(upro.ref[i], part)
        mask = jnp.concatenate([jnp.where(diag, kmask[i], 0.0)] * heads, axis=0) > 0.0
        expo = jnp.where(mask, jnp.exp(score * scale), 0.0)
        prob = expo / jnp.sum(expo, axis=1, keepdims=True)
        raw[i] = score
        probs[i] = prob
        prob_b = prob.astype(BF)
        mix = dot(prob_b, part).astype(BF)
        for h in range(heads):
            mixed[h, some[i], :] = mix[some[h], :]
        coef = fold_heads(prob_b, heads, fq, flen, 0) + fold_heads(selects[i], 1, fq, flen, 2 * heads)
        early[some[i], 2 * cols:2 * cols + 128] = coef.astype(BF)
    w_value = get(w_value)
    for h in range(heads):
        at = slice(h * HEAD, (h + 1) * HEAD)
        early[:, cols + h * HEAD:cols + (h + 1) * HEAD] = dot(mixed[h], w_value[:, at]).astype(BF)


def in_turn(m, ref, cols):
    return jnp.concatenate(
        [ref[:, pl.ds(pl.multiple_of((m ^ k) * cols, cols), cols)] for k in range(4)], axis=1
    )


def scores_kernel(flen, idx, normed, w_key, w_value, w_out, lmask, g0, g1, g23, early, probs, raw,
                  late, product, tpro, dscore, probs_b, mixed):
    m = idx[0]
    cols = w_key.ref.shape[1]
    heads = cols // HEAD
    rows = normed.ref.shape[0] // 4
    fq = rows // flen
    scale = 1.0 / HEAD**0.5
    diag = diagonal(fq, flen)
    some = [slice(i * fq, (i + 1) * fq) for i in range(4)]

    grads = jnp.concatenate([g[...] for g in (g0, g1, g23.at[0], g23.at[1])], axis=1)
    d_att = rdot(grads, in_turn(m, get(w_out), cols)).astype(BF)
    late[:, 0:cols] = d_att
    w_value = get(w_value)
    for h in range(heads):
        at = slice(h * HEAD, (h + 1) * HEAD)
        up = rdot(d_att[:, at], w_value[:, at]).astype(BF)
        for i in range(4):
            tpro.ref[i, some[h], :] = up[some[i], :]
    tpro.start()
    prods = []
    normed = get(normed)
    for i in range(4):
        part = normed[i * rows:(i + 1) * rows, :]
        d_prob = rdot(tpro.ref[i], part)
        prob = get(probs)[i]
        d_score = prob * (d_prob - jnp.sum(prob * d_prob, axis=1, keepdims=True)) * scale
        score_b = d_score.astype(BF)
        prob_b = prob.astype(BF)
        dscore[i] = score_b
        probs_b[i] = prob_b
        inner = d_score * get(raw)[i] + prob_b.astype(F32) * d_prob
        prods.append(jnp.sum(inner, axis=0, keepdims=True))
        mix = dot(score_b, part).astype(BF)
        for h in range(heads):
            mixed[h, some[i], :] = mix[some[h], :]
        coef = fold_heads(score_b, heads, fq, flen, heads)
        late[some[i], 2 * cols:2 * cols + 128] = coef.astype(BF)
    parts = []
    w_key = get(w_key)
    for h in range(heads):
        at = slice(h * HEAD, (h + 1) * HEAD)
        parts.append(dot(mixed[h], w_key[:, at]))
    d_query = jnp.concatenate(parts, axis=1).astype(BF)
    late[:, cols:2 * cols] = d_query
    inner = early[:, 0:cols].astype(F32) * d_query.astype(F32)
    inner = jnp.sum(inner, axis=1, keepdims=True)
    for i in range(4):
        select = jnp.where(diag, lmask[i], 0.0)
        product[i:i + 1, :] = prods[i] + jnp.sum(select * inner[some[i], :], axis=0, keepdims=True)


def normed_kernel(flen, idx, w_query, lmask, late, product, upro, tpro, dscore, probs_b, d0, d2, d1, d3, vpro):
    m = idx[0]
    rows = dscore.shape[2]
    fq = rows // flen
    cols = d0.shape[1]
    diag = diagonal(fq, flen)
    vpro[...] = rdot(late[:, cols:2 * cols], get(w_query)[...]).astype(BF)
    upro, tpro = get(upro), get(tpro)
    for i in range(4):
        select = jnp.where(diag, lmask[i], 0.0).astype(BF)
        left = jnp.concatenate([dscore[i], probs_b[i], select], axis=0)
        right = jnp.concatenate(
            [in_turn(m, upro.at[i], cols), in_turn(m, tpro.at[i], cols),
             in_turn(m, vpro.at[pl.ds(i * fq, fq), :], cols)], axis=0
        )
        total = tdot(left, right).astype(BF)
        for k, out in enumerate((d0, d1, d2, d3)):
            out[i * rows:(i + 1) * rows, :] = total[:, k * cols:(k + 1) * cols]
    for out in (d0, d1, d2, d3):
        out[4 * rows:4 * rows + 16, :] = jnp.zeros((16, cols), BF)
    for out in (d2, d3):
        out[4 * rows:4 * rows + 16, 0:rows] = jnp.concatenate(
            [product[...], jnp.zeros((12, rows), F32)], axis=0
        ).astype(BF)


def mix_rows(parts, flen, coefs, normed, z_all):
    fq = z_all.shape[1] // 16
    rows = fq * flen
    diag = jnp.where(diagonal(fq, flen), 1.0, 0.0)
    spread = jnp.concatenate([fold(p, rows, flen).T for p in parts], axis=1)
    for k, block in enumerate(normed):
        block = get(block)
        wide = dot(coefs[k], spread)
        for s in range(4):
            left = jnp.concatenate(
                [(wide[s * fq:(s + 1) * fq, j * rows:(j + 1) * rows] * diag).astype(BF)
                 for j in range(len(parts))], axis=0
            )
            mix = dot(left, block[s * rows:(s + 1) * rows, :]).astype(BF)
            for j in range(len(parts)):
                z_all[j, (k * 4 + s) * fq:(k * 4 + s + 1) * fq, :] = mix[j * fq:(j + 1) * fq, :]


def first_kernel(flen, heads, idx, b0, b1, b2, b3, e0, e1, e2, e3,
                 out_mine, out_other, z_value, z_last, z_all, att, all_grads):
    m, z, x = idx[0], idx[1], idx[2]
    early = (e0, e1, e2, e3)
    cols, half = out_mine.shape
    f_dev = e0.ref.shape[0]
    fq = f_dev // 4
    own = pl.ds(pl.multiple_of(x * half, half), half)
    far = pl.ds(pl.multiple_of((1 - x) * half, half), half)
    at = [pl.ds(pl.multiple_of((m ^ k) * fq, fq), fq) for k in range(4)]
    last = slice(2 * cols, 2 * cols + 128)
    coefs = [jnp.concatenate([get(e)[a, last] for e in early], axis=0) for a in at]
    mix_rows((*range(heads), 2 * heads), flen, coefs, (b0, b1, b2, b3), z_all)
    z_value.ref[...] = z_all[0:heads]
    z_last.ref[...] = z_all[heads]
    z_value.start()
    z_last.start()
    for k, rows in enumerate((b0, b1, b2, b3)):
        to = pl.ds(pl.multiple_of(((z ^ m) ^ k) * f_dev, f_dev), f_dev)
        all_grads[to, :] = get(rows)[4 * fq * flen:4 * fq * flen + f_dev, :]
    for s in range(4):
        att[s * f_dev:(s + 1) * f_dev, :] = get(early[s])[:, cols:2 * cols]
    out_mine[...] = tdot(att[...], all_grads[:, own])
    out_other[...] = tdot(att[...], all_grads[:, far]).astype(BF)


def value_kernel(heads, idx, z_value, z_last, l0, l1, l2, l3, value_mine, query_mine, other, d_all, dq_all):
    m, x = idx[0], idx[2]
    half, cols = value_mine.shape
    fq = l0.shape[0] // 4
    for k in range(4):
        a = pl.ds(pl.multiple_of((m ^ k) * fq, fq), fq)
        for s, late in enumerate((l0, l1, l2, l3)):
            to = slice((k * 4 + s) * fq, (k * 4 + s + 1) * fq)
            d_all[to, :] = late[a, 0:cols]
            dq_all[to, :] = late[a, cols:2 * cols]
    own = pl.ds(pl.multiple_of(x * half, half), half)
    far = pl.ds(pl.multiple_of((1 - x) * half, half), half)
    z_value, z_last = get(z_value), get(z_last)
    for h in range(heads):
        lanes = slice(h * HEAD, (h + 1) * HEAD)
        value_mine[:, lanes] = tdot(z_value[h, :, own], d_all[:, lanes])
        other[0, :, lanes] = tdot(z_value[h, :, far], d_all[:, lanes]).astype(BF)
    query_mine[...] = tdot(z_last[:, own], dq_all[...])
    other[1] = tdot(z_last[:, far], dq_all[...]).astype(BF)


def key_kernel(flen, heads, idx, b0, b1, b2, b3, *refs):
    early, late, refs = refs[:4], refs[4:8], refs[8:]
    mine, other, z_all, q_all = refs
    m, x = idx[0], idx[2]
    half, cols = mine.shape
    fq = late[0].ref.shape[0] // 4
    at = [pl.ds(pl.multiple_of((m ^ k) * fq, fq), fq) for k in range(4)]
    last = slice(2 * cols, 2 * cols + 128)
    coefs = [jnp.concatenate([get(item)[a, last] for item in late], axis=0) for a in at]
    mix_rows(range(heads, 2 * heads), flen, coefs, (b0, b1, b2, b3), z_all)
    for k, a in enumerate(at):
        for s in range(4):
            q_all[(k * 4 + s) * fq:(k * 4 + s + 1) * fq, :] = get(early[s])[a, 0:cols]
    own = pl.ds(pl.multiple_of(x * half, half), half)
    far = pl.ds(pl.multiple_of((1 - x) * half, half), half)
    for h in range(heads):
        lanes = slice(h * HEAD, (h + 1) * HEAD)
        mine[:, lanes] = tdot(z_all[h, :, own], q_all[:, lanes])
        other[:, lanes] = tdot(z_all[h, :, far], q_all[:, lanes]).astype(BF)


def on_device(tok_grad, occurrence, owned, token_ids, embeds, gain, w_query, w_key, w_value, w_out):
    n_tok = lax.axis_size("tok")
    n_out = n_tok // 2
    f_dev, flen = token_ids.shape
    width = gain.shape[0]
    cols = w_key.shape[1]
    rows = f_dev * flen
    feats = width // n_tok
    fq = f_dev // 4
    quarter = fq * flen
    heads = cols // HEAD
    m = lax.axis_index("mdl")
    t = lax.axis_index("tok")
    z, x = t // 2, t % 2
    idx = jnp.stack([m, z, x, t]).astype(jnp.int32)

    def flip(array, bit):
        return lax.ppermute(array, "mdl", [(i, i ^ bit) for i in range(4)])

    def swap(array):
        return lax.ppermute(array, "tok", [(i, i ^ 1) for i in range(n_tok)])

    def cross(array, k):
        return lax.ppermute(array, "tok", [(i, i ^ (2 * k)) for i in range(n_tok)])

    flat = embeds.reshape(rows, cols)
    flat2 = flip(flat, 2)

    owned_col = owned.reshape(-1, 1)
    occ_row = occurrence.reshape(1, -1)

    def sums(other, dtype, owners):
        return call(
            functools.partial(sums_kernel, n_out, other),
            (idx, owners, occ_row, tok_grad),
            [((n_out * f_dev, cols), dtype)],
            COSTS[0],
            later=(3,),
        )[0]

    give = sums(True, BF, owned_col)
    took = swap(give)
    keep = sums(False, F32, owned_col)
    flat2 = after(flat2, keep, when=TIES[11])
    flat1 = flip(flat, 1)
    own_sum, *pieces = call(
        add_kernel,
        (idx, keep, took),
        [((f_dev, cols), F32)] + [((f_dev, cols), BF)] * (n_out - 1),
        0.1,
    )
    came = [cross(piece, k) for k, piece in enumerate(pieces, 1)]
    flat2 = after(flat2, *pieces, when=TIES[23])
    flat3 = flip(flat2, 1)
    gain_row = gain.reshape(1, width)

    length = jnp.sum((token_ids != 0).astype(jnp.int32), axis=1)
    positions = jnp.arange(flen, dtype=jnp.int32)
    lastmask = (positions[None, :] == (length - 1)[:, None]).astype(F32)
    keymask = (positions[None, :] < length[:, None]).astype(F32)
    lmask = lastmask.reshape(4, 1, quarter)
    kmask = keymask.reshape(4, 1, quarter)

    sends = norm_quarter(idx, (flat, flat1, flat2, flat3), gain_row)
    far_rows = [cross(sends[k], k) for k in range(1, n_out)]

    item = ((f_dev, 2 * cols + 128), BF)
    square = (4, heads * fq, quarter)
    tall = ((4, heads * fq, width), BF)
    def sums_over_tok(*before):
        total = own_sum
        for piece in came:
            total = total + after(piece, *before).astype(F32)
        grad0 = total.astype(BF)
        grad1 = flip(grad0, 1)
        return grad0, grad1, flip(jnp.stack([grad0, grad1]), 2)

    if not TIES[18]:
        grad0, grad1, grad23 = sums_over_tok(sends[0])
    early, probs, raw, upro, normed, recip = call(
        functools.partial(forward_kernel, flen),
        (idx, flat, flat1, flat2, flat3, (after(gain_row, (grad0, grad23)[TIES[1] - 1]) if TIES[1] else gain_row), w_query, w_key, w_value, kmask, lmask),
        [item, (square, F32), (square, F32), tall, ((rows, width), BF), ((rows, 1), F32)],
        COSTS[2],
        [pltpu.VMEM((f_dev, width), BF), pltpu.VMEM((heads, f_dev, width), BF)],
        later=(1, 2, 3, 4, 6, 7, 8),
        sooner=(3, 4),
    )
    if TIES[18]:
        grad0, grad1, grad23 = sums_over_tok(early)
    pairs = []
    for a in range(n_out):
        for b in range(2):
            for c in range(4):
                pairs.append(((a * 2 + b) * 4 + c, (c * 2 + b) * 4 + a))
    turned = lax.ppermute(after(after(grad0, early, when=TIES[16]), grad23, when=TIES[19] > 1), ("tok", "mdl"), pairs)
    far_rows = [after(r, early, when=TIES[2]) for r in far_rows]
    turned = after(turned, early, when=TIES[2])
    sent = after(early, grad23, when=TIES[19])
    early1, early2 = cross(sent, 1), cross(sent, 2)
    gate1 = after(lmask, *far_rows, when=TIES[12])
    if TIES[17]:
        gate1 = after(gate1, early1)

    late, product, tpro, dscore, probs_b = call(
        functools.partial(scores_kernel, flen),
        (idx, normed, w_key, w_value, w_out, gate1, grad0, grad1, grad23, early, probs, raw),
        [item, ((4, quarter), F32), tall, (square, BF), (square, BF)],
        COSTS[4],
        [pltpu.VMEM((heads, f_dev, width), BF)],
        later=(4, 3, 1, 10, 11, 2),
        sooner=(2,),
    )
    if TIES[20]:
        early1, early2 = after(early1, late), after(early2, late)
    early_all = (early, early1, early2, cross(early2, 1) if TIES[10] else cross(early, 3))
    sent = after(late, early1, early2, when=TIES[21])
    late2 = cross(sent, 2)
    late13 = cross(jnp.stack([sent, late2]), 1)
    gate = after(lmask, late2, when=TIES[4])
    gate = after(gate, early_all[3], when=TIES[5])
    gate = after(gate, early1, early2, when=TIES[14])
    whole = jnp.concatenate([sends[0]] + far_rows + [turned])
    from2 = flip(after(whole, late, when=TIES[3]), 2)
    gate = after(gate, whole, when=TIES[15])
    d0, d2, d1, d3 = call(
        functools.partial(normed_kernel, flen),
        (idx, w_query, gate, late, product, upro, tpro, dscore, probs_b),
        [((rows + 16, cols), BF)] * 4,
        COSTS[5],
        [pltpu.VMEM((f_dev, width), BF)],
        later=(1, 5, 6),
    )
    beside = (flip(d1, 1), flip(d3, 1))
    from2 = after(from2, d0, when=TIES[6])
    normed_all = (whole, flip(whole, 1), from2, flip(from2, 1))
    across = (d2.astype(F32) + beside[1].astype(F32)).astype(BF)
    own = d0.astype(F32) + beside[0].astype(F32)

    late_all = (late, late13[0], late2, late13[1])


    f_all = n_out * f_dev
    out_mine, out_other, z_value, z_last = call(
        functools.partial(first_kernel, flen, heads),
        (after(idx, across, when=TIES[7]), *normed_all, *early_all),
        [((cols, feats), F32), ((cols, feats), BF), ((heads, f_all, 2 * feats), BF), ((f_all, 2 * feats), BF)],
        COSTS[6],
        [
            pltpu.VMEM((heads + 1, f_all, 2 * feats), BF),
            pltpu.VMEM((f_all, cols), BF),
            pltpu.VMEM((f_all, 2 * feats), BF),
        ],
        later=(5, 6, 7, 8, 1, 2, 3, 4),
        sooner=(2, 3),
    )
    out_grad = out_mine + swap(out_other).astype(F32)
    value_mine, query_mine, both_other = call(
        functools.partial(value_kernel, heads),
        (after(idx, out_grad, when=TIES[13]), z_value, z_last, *late_all),
        [((feats, cols), F32), ((feats, cols), F32), ((2, feats, cols), BF)],
        COSTS[7],
        [pltpu.VMEM((f_all, cols), BF), pltpu.VMEM((f_all, cols), BF)],
        later=(1, 2),
    )
    key_mine, key_other = call(
        functools.partial(key_kernel, flen, heads),
        (after(idx, both_other), *normed_all, *early_all, *late_all),
        [((feats, cols), F32), ((feats, cols), BF)],
        COSTS[8],
        [pltpu.VMEM((heads, f_all, 2 * feats), BF), pltpu.VMEM((f_all, cols), BF)],
        later=(9, 10, 11, 12, 1, 2, 3, 4, 5, 6, 7, 8),
    )
    came = after(swap(both_other), key_other, when=TIES[8])
    value_grad = value_mine + came[0].astype(F32)
    query_grad = query_mine + came[1].astype(F32)
    key_grad = key_mine + after(swap(key_other), value_grad, query_grad, out_grad, when=TIES[22]).astype(F32)

    crossed_over = after(flip(across, 2), key_other, when=TIES[9]).astype(F32)
    summed = own[0:rows] + crossed_over[0:rows]
    product = (across.astype(F32) + crossed_over)[rows:rows + 4, 0:quarter]
    gain_mine = lax.dynamic_slice_in_dim(gain, m * cols, cols, 0)
    scaled = summed.reshape(f_dev, flen, cols) * gain_mine
    recip = recip.reshape(f_dev, flen, 1)
    weight = recip * recip * (product.reshape(f_dev, flen, 1) * (1.0 / width))
    result = recip * scaled - embeds.astype(F32) * weight
    result = result + jnp.where(lastmask[..., None] > 0, grad0.astype(F32)[:, None, :], 0.0)
    return (result.astype(BF), query_grad, key_grad, value_grad, out_grad)


def general(tok_grad, occurrence, owned, token_ids, embeds, gain, w_query, w_key, w_value, w_out):
    f32 = F32
    bf16 = BF
    n_tok = lax.axis_size("tok")
    fgrams = owned.shape[0]
    f_dev = fgrams // n_tok
    width = gain.shape[0]
    cols = w_key.shape[1]
    local_heads = cols // HEAD
    flen = token_ids.shape[1]
    scale = 1.0 / HEAD**0.5
    onehot = (owned[:, None] == occurrence[None, :]).astype(bf16)
    partial_sum = jnp.dot(onehot, tok_grad, preferred_element_type=f32)
    blocks = partial_sum.reshape(n_tok, f_dev, tok_grad.shape[1])
    arrived = lax.all_to_all(blocks, "tok", split_axis=0, concat_axis=0, tiled=True)
    fgram_sum = jnp.sum(arrived, axis=0)
    fgram_grad = fgram_sum.astype(bf16)
    full_grad = lax.all_gather(fgram_grad, "mdl", axis=1, tiled=True)
    whole_embeds = lax.all_gather(embeds, "mdl", axis=2, tiled=True)
    length = jnp.sum((token_ids != 0).astype(jnp.int32), axis=1)
    positions = jnp.arange(flen, dtype=jnp.int32)
    lastmask = positions[None, :] == (length - 1)[:, None]
    keymask = (positions[None, :] < length[:, None]).astype(f32)
    xfull = whole_embeds.astype(f32)
    recip = lax.rsqrt(jnp.mean(xfull * xfull, axis=-1) + 1e-06)
    normed = (xfull * recip[..., None] * gain).astype(bf16)
    normed_last = jnp.sum(jnp.where(lastmask[..., None], normed.astype(f32), 0.0), axis=1).astype(bf16)
    rows = normed.reshape(f_dev * flen, width)
    keys = dot(rows, w_key).astype(bf16).reshape(f_dev, flen, local_heads, HEAD)
    values = dot(rows, w_value).astype(bf16).reshape(f_dev, flen, local_heads, HEAD)
    query = dot(normed_last, w_query).astype(bf16).reshape(f_dev, local_heads, HEAD)
    keys32 = keys.astype(f32)
    values32 = values.astype(f32)
    query32 = query.astype(f32)
    scores = jnp.einsum("fhd,fjhd->fhj", query, keys, preferred_element_type=f32) * scale
    expo = jnp.exp(scores) * keymask[:, None, :]
    probs = expo / jnp.sum(expo, axis=-1, keepdims=True)
    probs_b = probs.astype(bf16)
    attended = jnp.einsum("fhj,fjhd->fhd", probs_b, values, preferred_element_type=f32)
    attended = attended.astype(bf16).reshape(f_dev, cols)
    d_att = rdot(full_grad, w_out).reshape(f_dev, local_heads, HEAD)
    d_prob = jnp.einsum("fhd,fjhd->fhj", d_att, values32)
    d_score = probs * (d_prob - jnp.sum(probs * d_prob, axis=-1, keepdims=True)) * scale
    d_query = jnp.einsum("fhj,fjhd->fhd", d_score, keys32).astype(bf16).reshape(f_dev, cols)
    d_key = jnp.einsum("fhj,fhd->fjhd", d_score, query32).astype(bf16).reshape(f_dev * flen, cols)
    d_value = jnp.einsum("fhj,fhd->fjhd", probs_b.astype(f32), d_att)
    d_value = d_value.astype(bf16).reshape(f_dev * flen, cols)
    d_normed = (rdot(d_key, w_key) + rdot(d_value, w_value)).reshape(f_dev, flen, width)
    from_query = rdot(d_query, w_query)
    d_normed = d_normed + jnp.where(lastmask[..., None], from_query[:, None, :], 0.0)
    feat_start = lax.axis_index("mdl") * embeds.shape[2]
    summed = lax.psum(d_normed, "mdl")
    scaled = summed * gain
    product = jnp.mean(xfull * scaled, axis=-1)
    result = recip[..., None] * scaled - xfull * (recip**3 * product)[..., None]
    result = lax.dynamic_slice_in_dim(result, feat_start, embeds.shape[2], 2)
    result = result + jnp.where(lastmask[..., None], fgram_grad.astype(f32)[:, None, :], 0.0)
    query_grad, key_grad, value_grad = (
        lax.psum_scatter(part, "tok", scatter_dimension=0, tiled=True)
        for part in (tdot(normed_last, d_query), tdot(rows, d_key), tdot(rows, d_value))
    )
    out_grad = lax.psum_scatter(tdot(attended, full_grad), "tok", scatter_dimension=1, tiled=True)
    return (result.astype(bf16), query_grad, key_grad, value_grad, out_grad)


def chosen(*args):
    fits = lax.axis_size("tok") == 8 and lax.axis_size("mdl") == 4
    return (on_device if fits else general)(*args)


def solution(mesh):
    return jax.shard_map(
        chosen,
        mesh=mesh,
        in_specs=(
            P("tok", "mdl"),
            P("tok"),
            P(),
            P("tok", None),
            P("tok", None, "mdl"),
            P(),
            P(None, "mdl"),
            P(None, "mdl"),
            P(None, "mdl"),
            P("mdl", None),
        ),
        out_specs=(
            P("tok", None, "mdl"),
            P("tok", "mdl"),
            P("tok", "mdl"),
            P("tok", "mdl"),
            P("mdl", "tok"),
        ),
        check_vma=False,
    )
```

```python
import functools

import jax
import jax.numpy as jnp
from jax import lax
from jax.experimental import pallas as pl
from jax.experimental.pallas import tpu as pltpu
from jax.sharding import PartitionSpec as P

HEAD = 128
BF = jnp.bfloat16
F32 = jnp.float32
VMEM = pl.BlockSpec(memory_space=pltpu.VMEM)
SMEM = pl.BlockSpec(memory_space=pltpu.SMEM)
LIMIT = 56 * 2**20
SCALE = 1.15e9
COSTS = [0.1, 0.1, 0.1, 5, 0.1, 0.1, 5, 0.1, 0.1]
TIES = [1, 1, 1, 0, 1, 1, 0, 1, 1, 1, 1, 1, 0, 0, 1, 1, 0, 0, 0, 1, 0, 1, 1, 1]


def dot(left, right):
    return jnp.dot(left, right, preferred_element_type=F32)


def tdot(left, right):
    return lax.dot_general(left, right, (((0,), (0,)), ((), ())), preferred_element_type=F32)


def rdot(left, right):
    return lax.dot_general(left, right, (((1,), (1,)), ((), ())), preferred_element_type=F32)


def after(array, *others, when=True):
    return lax.optimization_barrier((array, *others))[0] if when else array


class Later:
    def __init__(self, copy, ref):
        self.copy, self.ref = copy, ref

    def get(self):
        if self.copy is not None:
            self.copy.wait()
            self.copy = None
        return self.ref


def get(ref):
    return ref.get() if isinstance(ref, Later) else ref


class Sooner:
    def __init__(self, copy, ref):
        self.copy, self.ref, self.started = copy, ref, False

    def start(self):
        self.copy.start()
        self.started = True


def call(body, ins, outs, micros, scratch=(), later=(), sooner=()):
    n_in, n_out, n_later, n_sooner = len(ins), len(outs), len(later), len(sooner)

    def kernel(*refs):
        given = list(refs[:n_in])
        made = list(refs[n_in:n_in + n_out])
        rest = refs[n_in + n_out:]
        buffers, rest = rest[:n_later + n_sooner], rest[n_later + n_sooner:]
        if buffers:
            sems, rest = rest[0], rest[1:]
        for j, i in enumerate(later):
            copy = pltpu.make_async_copy(given[i], buffers[j], sems.at[j])
            copy.start()
            given[i] = Later(copy, buffers[j])
        for j, i in enumerate(sooner):
            buffer = buffers[n_later + j]
            made[i] = Sooner(pltpu.make_async_copy(buffer, made[i], sems.at[n_later + j]), buffer)
        body(*given, *made, *rest)
        for i in later:
            given[i].get()
        for i in sooner:
            if not made[i].started:
                made[i].start()
        for i in sooner:
            made[i].copy.wait()

    in_specs, out_specs = [VMEM] * n_in, [VMEM] * n_out
    in_specs[0] = SMEM
    for i in later:
        in_specs[i] = pl.BlockSpec(memory_space=pl.ANY)
    for i in sooner:
        out_specs[i] = pl.BlockSpec(memory_space=pl.ANY)
    buffers = [pltpu.VMEM(ins[i].shape, ins[i].dtype) for i in later]
    buffers += [pltpu.VMEM(*outs[i]) for i in sooner]
    if buffers:
        buffers.append(pltpu.SemaphoreType.DMA((n_later + n_sooner,)))
    return pl.pallas_call(
        kernel,
        in_specs=in_specs,
        out_specs=out_specs,
        out_shape=[jax.ShapeDtypeStruct(s, t) for s, t in outs],
        scratch_shapes=[*buffers, *scratch],
        compiler_params=pltpu.CompilerParams(vmem_limit_bytes=LIMIT),
        cost_estimate=pl.CostEstimate(
            flops=int(micros * SCALE), bytes_accessed=0, transcendentals=0
        ),
    )(*ins)


def sums_kernel(n_out, other, idx, owned, occ, grads, out):
    z, x = idx[1], idx[2]
    f_dev = out.shape[0] // n_out
    side = 1 - x if other else x
    at = [pl.ds(pl.multiple_of(((z ^ k) * 2 + side) * f_dev, f_dev), f_dev) for k in range(n_out)]
    owners = jnp.concatenate([owned[a, :] for a in at], axis=0)
    onehot = jnp.where(owners == occ[...], 1.0, 0.0).astype(BF)
    out[...] = dot(onehot, get(grads)[...]).astype(out.dtype)


def add_kernel(idx, keep, took, own, *pieces):
    f_dev = own.shape[0]
    own[...] = keep[0:f_dev, :] + took[0:f_dev, :].astype(F32)
    for k, piece in enumerate(pieces, 1):
        at = slice(k * f_dev, (k + 1) * f_dev)
        piece[...] = (keep[at, :] + took[at, :].astype(F32)).astype(BF)


def norm_rows(m, tile, sources, gain, normed, recip):
    rows, cols = sources[0].shape
    width = 4 * cols

    def step(i, carry):
        at = pl.ds(pl.multiple_of(i * tile, tile), tile)
        total = jnp.zeros((tile, 1), F32)
        for block in sources:
            part = block[at, :].astype(F32)
            total = total + jnp.sum(part * part, axis=1, keepdims=True)
        r = lax.rsqrt(total * (1.0 / width) + 1e-06)
        if recip is not None:
            recip[at, :] = r
        for k, block in enumerate(sources):
            lanes = pl.ds(pl.multiple_of((m ^ k) * cols, cols), cols)
            normed[at, lanes] = (block[at, :].astype(F32) * r * gain[:, lanes]).astype(BF)
        return carry

    lax.fori_loop(0, rows // tile, step, 0, unroll=True)


def quarter_kernel(idx, x0, x1, x2, x3, gain, *refs):
    sends, normed = refs[:-1], refs[-1]
    m, z = idx[0], idx[1]
    cols = x0.shape[1]
    norm_rows(m, 32, (x0, x1, x2, x3), gain, normed, None)
    for k, send in enumerate(sends):
        send[...] = normed[:, pl.ds(pl.multiple_of((z ^ k) * cols, cols), cols)]


def norm_quarter(idx, blocks, gain):
    rows, cols = blocks[0].shape
    width = 4 * cols
    quarter = rows // 4
    return pl.pallas_call(
        quarter_kernel,
        grid_spec=pltpu.PrefetchScalarGridSpec(
            num_scalar_prefetch=1,
            grid=(1,),
            in_specs=[pl.BlockSpec((quarter, cols), lambda i, idx: (idx[0], 0))] * 4
            + [pl.BlockSpec((1, width), lambda i, idx: (0, 0))],
            out_specs=[pl.BlockSpec((quarter, cols), lambda i, idx: (0, 0))] * 4,
            scratch_shapes=[pltpu.VMEM((quarter, width), BF)],
        ),
        out_shape=[jax.ShapeDtypeStruct((quarter, cols), BF)] * 4,
        compiler_params=pltpu.CompilerParams(vmem_limit_bytes=LIMIT),
        cost_estimate=pl.CostEstimate(flops=int(COSTS[1] * SCALE), bytes_accessed=0, transcendentals=0),
    )(idx, *blocks, gain)


def diagonal(f_quarter, flen):
    rows = lax.broadcasted_iota(jnp.int32, (f_quarter, f_quarter * flen), 0)
    lanes = lax.broadcasted_iota(jnp.int32, (f_quarter, f_quarter * flen), 1)
    return rows == lanes // flen


def fold(which, lanes, flen):
    rows = lax.broadcasted_iota(jnp.int32, (lanes, 128), 0)
    to = lax.broadcasted_iota(jnp.int32, (lanes, 128), 1)
    return jnp.where(to == lax.rem(rows, flen) + which * flen, 1.0, 0.0).astype(BF)


def fold_heads(values, heads, fq, flen, shift):
    lanes = lax.broadcasted_iota(jnp.int32, (heads * fq, 128), 1)
    rows = lax.broadcasted_iota(jnp.int32, (heads * fq, 128), 0)
    back = lax.broadcasted_iota(jnp.int32, (fq * flen, 128), 0)
    to = lax.broadcasted_iota(jnp.int32, (fq * flen, 128), 1)
    every = jnp.where(lax.rem(back, flen) == lax.rem(to, flen), 1.0, 0.0).astype(BF)
    wide = jnp.where(lanes // flen == rows // fq + shift, dot(values, every), 0.0)
    total = wide[0:fq]
    for h in range(1, heads):
        total = total + wide[h * fq:(h + 1) * fq]
    return total


def forward_kernel(flen, idx, x0, x1, x2, x3, gain, w_query, w_key, w_value, kmask, lmask,
                   early, probs, raw, upro, normed_out, recip, last, mixed):
    m = idx[0]
    cols = w_query.ref.shape[1]
    heads = cols // HEAD
    normed = normed_out.ref
    rows = normed.shape[0] // 4
    fq = rows // flen
    scale = 1.0 / HEAD**0.5
    diag = diagonal(fq, flen)
    some = [slice(i * fq, (i + 1) * fq) for i in range(4)]

    norm_rows(m, 32, [get(x) for x in (x0, x1, x2, x3)], gain, normed, recip)
    normed_out.start()
    selects = [jnp.where(diag, lmask[i], 0.0).astype(BF) for i in range(4)]
    for i in range(4):
        last[some[i], :] = dot(selects[i], normed[i * rows:(i + 1) * rows, :]).astype(BF)
    query = dot(last[...], get(w_query)[...]).astype(BF)
    early[:, 0:cols] = query
    w_key = get(w_key)
    for h in range(heads):
        at = slice(h * HEAD, (h + 1) * HEAD)
        up = rdot(query[:, at], w_key[:, at]).astype(BF)
        for i in range(4):
            upro.ref[i, some[h], :] = up[some[i], :]
    upro.start()
    for i in range(4):
        part = normed[i * rows:(i + 1) * rows, :]
        score = rdot(upro.ref[i], part)
        mask = jnp.concatenate([jnp.where(diag, kmask[i], 0.0)] * heads, axis=0) > 0.0
        expo = jnp.where(mask, jnp.exp(score * scale), 0.0)
        prob = expo / jnp.sum(expo, axis=1, keepdims=True)
        raw[i] = score
        probs[i] = prob
        prob_b = prob.astype(BF)
        mix = dot(prob_b, part).astype(BF)
        for h in range(heads):
            mixed[h, some[i], :] = mix[some[h], :]
        coef = fold_heads(prob_b, heads, fq, flen, 0) + fold_heads(selects[i], 1, fq, flen, 2 * heads)
        early[some[i], 2 * cols:2 * cols + 128] = coef.astype(BF)
    w_value = get(w_value)
    for h in range(heads):
        at = slice(h * HEAD, (h + 1) * HEAD)
        early[:, cols + h * HEAD:cols + (h + 1) * HEAD] = dot(mixed[h], w_value[:, at]).astype(BF)


def in_turn(m, ref, cols):
    return jnp.concatenate(
        [ref[:, pl.ds(pl.multiple_of((m ^ k) * cols, cols), cols)] for k in range(4)], axis=1
    )


def scores_kernel(flen, idx, normed, w_key, w_value, w_out, lmask, g0, g1, g23, early, probs, raw,
                  late, product, tpro, dscore, probs_b, mixed):
    m = idx[0]
    cols = w_key.ref.shape[1]
    heads = cols // HEAD
    rows = normed.ref.shape[0] // 4
    fq = rows // flen
    scale = 1.0 / HEAD**0.5
    diag = diagonal(fq, flen)
    some = [slice(i * fq, (i + 1) * fq) for i in range(4)]

    grads = jnp.concatenate([g[...] for g in (g0, g1, g23.at[0], g23.at[1])], axis=1)
    d_att = rdot(grads, in_turn(m, get(w_out), cols)).astype(BF)
    late[:, 0:cols] = d_att
    w_value = get(w_value)
    for h in range(heads):
        at = slice(h * HEAD, (h + 1) * HEAD)
        up = rdot(d_att[:, at], w_value[:, at]).astype(BF)
        for i in range(4):
            tpro.ref[i, some[h], :] = up[some[i], :]
    tpro.start()
    prods = []
    normed = get(normed)
    for i in range(4):
        part = normed[i * rows:(i + 1) * rows, :]
        d_prob = rdot(tpro.ref[i], part)
        prob = get(probs)[i]
        d_score = prob * (d_prob - jnp.sum(prob * d_prob, axis=1, keepdims=True)) * scale
        score_b = d_score.astype(BF)
        prob_b = prob.astype(BF)
        dscore[i] = score_b
        probs_b[i] = prob_b
        inner = d_score * get(raw)[i] + prob_b.astype(F32) * d_prob
        prods.append(jnp.sum(inner, axis=0, keepdims=True))
        mix = dot(score_b, part).astype(BF)
        for h in range(heads):
            mixed[h, some[i], :] = mix[some[h], :]
        coef = fold_heads(score_b, heads, fq, flen, heads)
        late[some[i], 2 * cols:2 * cols + 128] = coef.astype(BF)
    parts = []
    w_key = get(w_key)
    for h in range(heads):
        at = slice(h * HEAD, (h + 1) * HEAD)
        parts.append(dot(mixed[h], w_key[:, at]))
    d_query = jnp.concatenate(parts, axis=1).astype(BF)
    late[:, cols:2 * cols] = d_query
    inner = early[:, 0:cols].astype(F32) * d_query.astype(F32)
    inner = jnp.sum(inner, axis=1, keepdims=True)
    for i in range(4):
        select = jnp.where(diag, lmask[i], 0.0)
        product[i:i + 1, :] = prods[i] + jnp.sum(select * inner[some[i], :], axis=0, keepdims=True)


def normed_kernel(flen, idx, w_query, lmask, late, product, upro, tpro, dscore, probs_b, d0, d2, d1, d3, vpro):
    m = idx[0]
    rows = dscore.shape[2]
    fq = rows // flen
    cols = d0.shape[1]
    diag = diagonal(fq, flen)
    vpro[...] = rdot(late[:, cols:2 * cols], get(w_query)[...]).astype(BF)
    upro, tpro = get(upro), get(tpro)
    for i in range(4):
        select = jnp.where(diag, lmask[i], 0.0).astype(BF)
        left = jnp.concatenate([dscore[i], probs_b[i], select], axis=0)
        right = jnp.concatenate(
            [in_turn(m, upro.at[i], cols), in_turn(m, tpro.at[i], cols),
             in_turn(m, vpro.at[pl.ds(i * fq, fq), :], cols)], axis=0
        )
        total = tdot(left, right).astype(BF)
        for k, out in enumerate((d0, d1, d2, d3)):
            out[i * rows:(i + 1) * rows, :] = total[:, k * cols:(k + 1) * cols]
    for out in (d0, d1, d2, d3):
        out[4 * rows:4 * rows + 16, :] = jnp.zeros((16, cols), BF)
    for out in (d2, d3):
        out[4 * rows:4 * rows + 16, 0:rows] = jnp.concatenate(
            [product[...], jnp.zeros((12, rows), F32)], axis=0
        ).astype(BF)


def mix_rows(parts, flen, coefs, normed, z_all):
    fq = z_all.shape[1] // 16
    rows = fq * flen
    diag = jnp.where(diagonal(fq, flen), 1.0, 0.0)
    spread = jnp.concatenate([fold(p, rows, flen).T for p in parts], axis=1)
    for k, block in enumerate(normed):
        block = get(block)
        wide = dot(coefs[k], spread)
        for s in range(4):
            left = jnp.concatenate(
                [(wide[s * fq:(s + 1) * fq, j * rows:(j + 1) * rows] * diag).astype(BF)
                 for j in range(len(parts))], axis=0
            )
            mix = dot(left, block[s * rows:(s + 1) * rows, :]).astype(BF)
            for j in range(len(parts)):
                z_all[j, (k * 4 + s) * fq:(k * 4 + s + 1) * fq, :] = mix[j * fq:(j + 1) * fq, :]


def first_kernel(flen, heads, idx, b0, b1, b2, b3, e0, e1, e2, e3,
                 out_mine, out_other, z_value, z_last, z_all, att, all_grads):
    m, z, x = idx[0], idx[1], idx[2]
    early = (e0, e1, e2, e3)
    cols, half = out_mine.shape
    f_dev = e0.ref.shape[0]
    fq = f_dev // 4
    own = pl.ds(pl.multiple_of(x * half, half), half)
    far = pl.ds(pl.multiple_of((1 - x) * half, half), half)
    at = [pl.ds(pl.multiple_of((m ^ k) * fq, fq), fq) for k in range(4)]
    last = slice(2 * cols, 2 * cols + 128)
    coefs = [jnp.concatenate([get(e)[a, last] for e in early], axis=0) for a in at]
    mix_rows((*range(heads), 2 * heads), flen, coefs, (b0, b1, b2, b3), z_all)
    z_value.ref[...] = z_all[0:heads]
    z_last.ref[...] = z_all[heads]
    z_value.start()
    z_last.start()
    for k, rows in enumerate((b0, b1, b2, b3)):
        to = pl.ds(pl.multiple_of(((z ^ m) ^ k) * f_dev, f_dev), f_dev)
        all_grads[to, :] = get(rows)[4 * fq * flen:4 * fq * flen + f_dev, :]
    for s in range(4):
        att[s * f_dev:(s + 1) * f_dev, :] = get(early[s])[:, cols:2 * cols]
    out_mine[...] = tdot(att[...], all_grads[:, own])
    out_other[...] = tdot(att[...], all_grads[:, far]).astype(BF)


def value_kernel(heads, idx, z_value, z_last, l0, l2, l13, value_mine, query_mine, other, d_all, dq_all):
    m, x = idx[0], idx[2]
    l1, l3 = l13.at[0], l13.at[1]
    half, cols = value_mine.shape
    fq = l0.shape[0] // 4
    for k in range(4):
        a = pl.ds(pl.multiple_of((m ^ k) * fq, fq), fq)
        for s, late in enumerate((l0, l1, l2, l3)):
            to = slice((k * 4 + s) * fq, (k * 4 + s + 1) * fq)
            d_all[to, :] = late[a, 0:cols]
            dq_all[to, :] = late[a, cols:2 * cols]
    own = pl.ds(pl.multiple_of(x * half, half), half)
    far = pl.ds(pl.multiple_of((1 - x) * half, half), half)
    z_value, z_last = get(z_value), get(z_last)
    for h in range(heads):
        lanes = slice(h * HEAD, (h + 1) * HEAD)
        value_mine[:, lanes] = tdot(z_value[h, :, own], d_all[:, lanes])
        other[0, :, lanes] = tdot(z_value[h, :, far], d_all[:, lanes]).astype(BF)
    query_mine[...] = tdot(z_last[:, own], dq_all[...])
    other[1] = tdot(z_last[:, far], dq_all[...]).astype(BF)


def key_kernel(flen, heads, idx, b0, b1, b2, b3, *refs):
    early, late, refs = refs[:4], [get(r) for r in refs[4:7]], refs[7:]
    late = [late[0], late[2].at[0], late[1], late[2].at[1]]
    mine, other, z_all, q_all = refs
    m, x = idx[0], idx[2]
    half, cols = mine.shape
    fq = late[0].shape[0] // 4
    at = [pl.ds(pl.multiple_of((m ^ k) * fq, fq), fq) for k in range(4)]
    last = slice(2 * cols, 2 * cols + 128)
    coefs = [jnp.concatenate([get(item)[a, last] for item in late], axis=0) for a in at]
    mix_rows(range(heads, 2 * heads), flen, coefs, (b0, b1, b2, b3), z_all)
    for k, a in enumerate(at):
        for s in range(4):
            q_all[(k * 4 + s) * fq:(k * 4 + s + 1) * fq, :] = get(early[s])[a, 0:cols]
    own = pl.ds(pl.multiple_of(x * half, half), half)
    far = pl.ds(pl.multiple_of((1 - x) * half, half), half)
    for h in range(heads):
        lanes = slice(h * HEAD, (h + 1) * HEAD)
        mine[:, lanes] = tdot(z_all[h, :, own], q_all[:, lanes])
        other[:, lanes] = tdot(z_all[h, :, far], q_all[:, lanes]).astype(BF)


def on_device(tok_grad, occurrence, owned, token_ids, embeds, gain, w_query, w_key, w_value, w_out):
    n_tok = lax.axis_size("tok")
    n_out = n_tok // 2
    f_dev, flen = token_ids.shape
    width = gain.shape[0]
    cols = w_key.shape[1]
    rows = f_dev * flen
    feats = width // n_tok
    fq = f_dev // 4
    quarter = fq * flen
    heads = cols // HEAD
    m = lax.axis_index("mdl")
    t = lax.axis_index("tok")
    z, x = t // 2, t % 2
    idx = jnp.stack([m, z, x, t]).astype(jnp.int32)

    def flip(array, bit):
        return lax.ppermute(array, "mdl", [(i, i ^ bit) for i in range(4)])

    def swap(array):
        return lax.ppermute(array, "tok", [(i, i ^ 1) for i in range(n_tok)])

    def cross(array, k):
        return lax.ppermute(array, "tok", [(i, i ^ (2 * k)) for i in range(n_tok)])

    flat = embeds.reshape(rows, cols)
    flat2 = flip(flat, 2)

    owned_col = owned.reshape(-1, 1)
    occ_row = occurrence.reshape(1, -1)

    def sums(other, dtype, owners):
        return call(
            functools.partial(sums_kernel, n_out, other),
            (idx, owners, occ_row, tok_grad),
            [((n_out * f_dev, cols), dtype)],
            COSTS[0],
            later=(3,),
        )[0]

    give = sums(True, BF, owned_col)
    took = swap(give)
    keep = sums(False, F32, owned_col)
    flat2 = after(flat2, keep, when=TIES[11])
    flat1 = flip(flat, 1)
    own_sum, *pieces = call(
        add_kernel,
        (idx, keep, took),
        [((f_dev, cols), F32)] + [((f_dev, cols), BF)] * (n_out - 1),
        0.1,
    )
    came = [cross(piece, k) for k, piece in enumerate(pieces, 1)]
    flat2 = after(flat2, *pieces, when=TIES[23])
    flat3 = flip(flat2, 1)
    gain_row = gain.reshape(1, width)

    length = jnp.sum((token_ids != 0).astype(jnp.int32), axis=1)
    positions = jnp.arange(flen, dtype=jnp.int32)
    lastmask = (positions[None, :] == (length - 1)[:, None]).astype(F32)
    keymask = (positions[None, :] < length[:, None]).astype(F32)
    lmask = lastmask.reshape(4, 1, quarter)
    kmask = keymask.reshape(4, 1, quarter)

    sends = norm_quarter(idx, (flat, flat1, flat2, flat3), gain_row)
    far_rows = [cross(sends[k], k) for k in range(1, n_out)]

    item = ((f_dev, 2 * cols + 128), BF)
    square = (4, heads * fq, quarter)
    tall = ((4, heads * fq, width), BF)
    def sums_over_tok(*before):
        total = own_sum
        for piece in came:
            total = total + after(piece, *before).astype(F32)
        grad0 = total.astype(BF)
        grad1 = flip(grad0, 1)
        return grad0, grad1, flip(jnp.stack([grad0, grad1]), 2)

    if not TIES[18]:
        grad0, grad1, grad23 = sums_over_tok(sends[0])
    early, probs, raw, upro, normed, recip = call(
        functools.partial(forward_kernel, flen),
        (idx, flat, flat1, flat2, flat3, (after(gain_row, (grad0, grad23)[TIES[1] - 1]) if TIES[1] else gain_row), w_query, w_key, w_value, kmask, lmask),
        [item, (square, F32), (square, F32), tall, ((rows, width), BF), ((rows, 1), F32)],
        COSTS[2],
        [pltpu.VMEM((f_dev, width), BF), pltpu.VMEM((heads, f_dev, width), BF)],
        later=(1, 2, 3, 4, 6, 7, 8),
        sooner=(3, 4),
    )
    if TIES[18]:
        grad0, grad1, grad23 = sums_over_tok(early)
    pairs = []
    for a in range(n_out):
        for b in range(2):
            for c in range(4):
                pairs.append(((a * 2 + b) * 4 + c, (c * 2 + b) * 4 + a))
    turned = lax.ppermute(after(after(grad0, early, when=TIES[16]), grad23, when=TIES[19] > 1), ("tok", "mdl"), pairs)
    far_rows = [after(r, early, when=TIES[2]) for r in far_rows]
    turned = after(turned, early, when=TIES[2])
    sent = after(early, grad23, when=TIES[19])
    early1, early2 = cross(sent, 1), cross(sent, 2)
    gate1 = after(lmask, *far_rows, when=TIES[12])
    if TIES[17]:
        gate1 = after(gate1, early1)

    late, product, tpro, dscore, probs_b = call(
        functools.partial(scores_kernel, flen),
        (idx, normed, w_key, w_value, w_out, gate1, grad0, grad1, grad23, early, probs, raw),
        [item, ((4, quarter), F32), tall, (square, BF), (square, BF)],
        COSTS[4],
        [pltpu.VMEM((heads, f_dev, width), BF)],
        later=(4, 3, 1, 10, 11, 2),
        sooner=(2,),
    )
    if TIES[20]:
        early1, early2 = after(early1, late), after(early2, late)
    early_all = (early, early1, early2, cross(early2, 1) if TIES[10] else cross(early, 3))
    sent = after(late, early1, early2, when=TIES[21])
    late2 = cross(sent, 2)
    late13 = cross(jnp.stack([sent, late2]), 1)
    gate = after(lmask, late2, when=TIES[4])
    gate = after(gate, early_all[3], when=TIES[5])
    gate = after(gate, early1, early2, when=TIES[14])
    whole = jnp.concatenate([sends[0]] + far_rows + [turned])
    from2 = flip(after(whole, late, when=TIES[3]), 2)
    gate = after(gate, whole, when=TIES[15])
    d0, d2, d1, d3 = call(
        functools.partial(normed_kernel, flen),
        (idx, w_query, gate, late, product, upro, tpro, dscore, probs_b),
        [((rows + 16, cols), BF)] * 4,
        COSTS[5],
        [pltpu.VMEM((f_dev, width), BF)],
        later=(1, 5, 6),
    )
    beside = (flip(d1, 1), flip(d3, 1))
    from2 = after(from2, d0, when=TIES[6])
    normed_all = (whole, flip(whole, 1), from2, flip(from2, 1))
    across = (d2.astype(F32) + beside[1].astype(F32)).astype(BF)
    own = d0.astype(F32) + beside[0].astype(F32)

    late_all = (late, late2, late13)


    f_all = n_out * f_dev
    out_mine, out_other, z_value, z_last = call(
        functools.partial(first_kernel, flen, heads),
        (after(idx, across, when=TIES[7]), *normed_all, *early_all),
        [((cols, feats), F32), ((cols, feats), BF), ((heads, f_all, 2 * feats), BF), ((f_all, 2 * feats), BF)],
        COSTS[6],
        [
            pltpu.VMEM((heads + 1, f_all, 2 * feats), BF),
            pltpu.VMEM((f_all, cols), BF),
            pltpu.VMEM((f_all, 2 * feats), BF),
        ],
        later=(5, 6, 7, 8, 1, 2, 3, 4),
        sooner=(2, 3),
    )
    out_grad = out_mine + swap(out_other).astype(F32)
    value_mine, query_mine, both_other = call(
        functools.partial(value_kernel, heads),
        (after(idx, out_grad, when=TIES[13]), z_value, z_last, *late_all),
        [((feats, cols), F32), ((feats, cols), F32), ((2, feats, cols), BF)],
        COSTS[7],
        [pltpu.VMEM((f_all, cols), BF), pltpu.VMEM((f_all, cols), BF)],
        later=(1, 2),
    )
    key_mine, key_other = call(
        functools.partial(key_kernel, flen, heads),
        (after(idx, both_other), *normed_all, *early_all, *late_all),
        [((feats, cols), F32), ((feats, cols), BF)],
        COSTS[8],
        [pltpu.VMEM((heads, f_all, 2 * feats), BF), pltpu.VMEM((f_all, cols), BF)],
        later=(9, 10, 11, 1, 2, 3, 4, 5, 6, 7, 8),
    )
    came = after(swap(both_other), key_other, when=TIES[8])
    value_grad = value_mine + came[0].astype(F32)
    query_grad = query_mine + came[1].astype(F32)
    key_grad = key_mine + after(swap(key_other), value_grad, query_grad, out_grad, when=TIES[22]).astype(F32)

    crossed_over = after(flip(across, 2), key_other, when=TIES[9]).astype(F32)
    summed = own[0:rows] + crossed_over[0:rows]
    product = (across.astype(F32) + crossed_over)[rows:rows + 4, 0:quarter]
    gain_mine = lax.dynamic_slice_in_dim(gain, m * cols, cols, 0)
    scaled = summed.reshape(f_dev, flen, cols) * gain_mine
    recip = recip.reshape(f_dev, flen, 1)
    weight = recip * recip * (product.reshape(f_dev, flen, 1) * (1.0 / width))
    result = recip * scaled - embeds.astype(F32) * weight
    result = result + jnp.where(lastmask[..., None] > 0, grad0.astype(F32)[:, None, :], 0.0)
    return (result.astype(BF), query_grad, key_grad, value_grad, out_grad)


def general(tok_grad, occurrence, owned, token_ids, embeds, gain, w_query, w_key, w_value, w_out):
    f32 = F32
    bf16 = BF
    n_tok = lax.axis_size("tok")
    fgrams = owned.shape[0]
    f_dev = fgrams // n_tok
    width = gain.shape[0]
    cols = w_key.shape[1]
    local_heads = cols // HEAD
    flen = token_ids.shape[1]
    scale = 1.0 / HEAD**0.5
    onehot = (owned[:, None] == occurrence[None, :]).astype(bf16)
    partial_sum = jnp.dot(onehot, tok_grad, preferred_element_type=f32)
    blocks = partial_sum.reshape(n_tok, f_dev, tok_grad.shape[1])
    arrived = lax.all_to_all(blocks, "tok", split_axis=0, concat_axis=0, tiled=True)
    fgram_sum = jnp.sum(arrived, axis=0)
    fgram_grad = fgram_sum.astype(bf16)
    full_grad = lax.all_gather(fgram_grad, "mdl", axis=1, tiled=True)
    whole_embeds = lax.all_gather(embeds, "mdl", axis=2, tiled=True)
    length = jnp.sum((token_ids != 0).astype(jnp.int32), axis=1)
    positions = jnp.arange(flen, dtype=jnp.int32)
    lastmask = positions[None, :] == (length - 1)[:, None]
    keymask = (positions[None, :] < length[:, None]).astype(f32)
    xfull = whole_embeds.astype(f32)
    recip = lax.rsqrt(jnp.mean(xfull * xfull, axis=-1) + 1e-06)
    normed = (xfull * recip[..., None] * gain).astype(bf16)
    normed_last = jnp.sum(jnp.where(lastmask[..., None], normed.astype(f32), 0.0), axis=1).astype(bf16)
    rows = normed.reshape(f_dev * flen, width)
    keys = dot(rows, w_key).astype(bf16).reshape(f_dev, flen, local_heads, HEAD)
    values = dot(rows, w_value).astype(bf16).reshape(f_dev, flen, local_heads, HEAD)
    query = dot(normed_last, w_query).astype(bf16).reshape(f_dev, local_heads, HEAD)
    keys32 = keys.astype(f32)
    values32 = values.astype(f32)
    query32 = query.astype(f32)
    scores = jnp.einsum("fhd,fjhd->fhj", query, keys, preferred_element_type=f32) * scale
    expo = jnp.exp(scores) * keymask[:, None, :]
    probs = expo / jnp.sum(expo, axis=-1, keepdims=True)
    probs_b = probs.astype(bf16)
    attended = jnp.einsum("fhj,fjhd->fhd", probs_b, values, preferred_element_type=f32)
    attended = attended.astype(bf16).reshape(f_dev, cols)
    d_att = rdot(full_grad, w_out).reshape(f_dev, local_heads, HEAD)
    d_prob = jnp.einsum("fhd,fjhd->fhj", d_att, values32)
    d_score = probs * (d_prob - jnp.sum(probs * d_prob, axis=-1, keepdims=True)) * scale
    d_query = jnp.einsum("fhj,fjhd->fhd", d_score, keys32).astype(bf16).reshape(f_dev, cols)
    d_key = jnp.einsum("fhj,fhd->fjhd", d_score, query32).astype(bf16).reshape(f_dev * flen, cols)
    d_value = jnp.einsum("fhj,fhd->fjhd", probs_b.astype(f32), d_att)
    d_value = d_value.astype(bf16).reshape(f_dev * flen, cols)
    d_normed = (rdot(d_key, w_key) + rdot(d_value, w_value)).reshape(f_dev, flen, width)
    from_query = rdot(d_query, w_query)
    d_normed = d_normed + jnp.where(lastmask[..., None], from_query[:, None, :], 0.0)
    feat_start = lax.axis_index("mdl") * embeds.shape[2]
    summed = lax.psum(d_normed, "mdl")
    scaled = summed * gain
    product = jnp.mean(xfull * scaled, axis=-1)
    result = recip[..., None] * scaled - xfull * (recip**3 * product)[..., None]
    result = lax.dynamic_slice_in_dim(result, feat_start, embeds.shape[2], 2)
    result = result + jnp.where(lastmask[..., None], fgram_grad.astype(f32)[:, None, :], 0.0)
    query_grad, key_grad, value_grad = (
        lax.psum_scatter(part, "tok", scatter_dimension=0, tiled=True)
        for part in (tdot(normed_last, d_query), tdot(rows, d_key), tdot(rows, d_value))
    )
    out_grad = lax.psum_scatter(tdot(attended, full_grad), "tok", scatter_dimension=1, tiled=True)
    return (result.astype(bf16), query_grad, key_grad, value_grad, out_grad)


def chosen(*args):
    fits = lax.axis_size("tok") == 8 and lax.axis_size("mdl") == 4
    return (on_device if fits else general)(*args)


def solution(mesh):
    return jax.shard_map(
        chosen,
        mesh=mesh,
        in_specs=(
            P("tok", "mdl"),
            P("tok"),
            P(),
            P("tok", None),
            P("tok", None, "mdl"),
            P(),
            P(None, "mdl"),
            P(None, "mdl"),
            P(None, "mdl"),
            P("mdl", None),
        ),
        out_specs=(
            P("tok", None, "mdl"),
            P("tok", "mdl"),
            P("tok", "mdl"),
            P("tok", "mdl"),
            P("mdl", "tok"),
        ),
        check_vma=False,
    )
```
